32 devices in a mesh: ctx: 16 (over z, y, core), ch: 2 (over x).
Axes of the slice: x: 2, y: 2, z: 4, core: 2. Of those that a mesh axis runs over, the one named last changes fastest.
Arguments:
- x_one: bfloat16 [2048, 4096], P('ctx', 'ch'), may hold values from -6 to 6
- x_two: bfloat16 [2048, 4096], P('ctx', 'ch'), may hold values from -6 to 6
- values: bfloat16 [2048, 4096], P('ctx', 'ch'), may hold values from -6 to 6
- grad_out: bfloat16 [2048, 4096], P('ctx', 'ch'), may hold values from -3 to 3
- filter_raw: bfloat16 [1024, 512], P('ctx', 'ch'), may hold values from -4 to 4
Outputs:
- grad_x_one: bfloat16 [2048, 4096], P('ctx', 'ch')
- grad_x_two: bfloat16 [2048, 4096], P('ctx', 'ch')
- grad_values: bfloat16 [2048, 4096], P('ctx', 'ch')
- grad_filter: float32 [1024, 512], P('ctx', 'ch')
The draws below stay inside these ranges and needn't reach their ends.
All inputs are finite; a program needn't handle non-finite values.
Results may differ from the reference program's by a relative error of at most 0.0049.
Values may be sent and summed in bfloat16 or wider, within the bound.
No kernel may reach another device: no remote copies, remote signals or barrier semaphores. Data moves between devices by JAX's collectives and lax.ppermute only.
A program may use at most 192 MiB of HBM per device.

```python
import math
import jax
import jax.numpy as jnp
from jax import lax

C = 4096
F = 512
L = 1024
TOKENS = 2048


def shard_levels(rng, dims, split, least, largest):
    gain = 1.0
    for axis_at, shards_of in split:
        draws = jax.random.uniform(jax.random.fold_in(jax.random.fold_in(rng, 6), axis_at), (shards_of,), jnp.float32, least / len(split), largest / len(split))
        gain = gain * jnp.repeat(jnp.exp(draws), dims[axis_at] // shards_of).reshape((-1,) + (1,) * (len(dims) - 1 - axis_at))
    return gain


def noise(stream_key, dims, width, reach, shards=(), kind=jnp.bfloat16):
    drawn = jax.random.normal(stream_key, dims, jnp.float32) * width
    if len(shards) > 0:
        drawn = shard_levels(stream_key, dims, shards, -0.22, 0.18) * drawn
    return jnp.clip(drawn, min=-reach, max=reach).astype(kind)


def setup_inputs(seed: int = 0) -> dict:
    splits = jax.random.split(jax.random.key(seed), 6)
    return {
        "x_one": noise(splits[0], (TOKENS, C), 1.0, 6.0, ((0, 16), (1, 2))),
        "x_two": noise(splits[1], (TOKENS, C), 1.0, 6.0, ((0, 16), (1, 2))),
        "values": noise(splits[2], (TOKENS, C), 1.0, 6.0, ((0, 16), (1, 2))),
        "grad_out": noise(splits[3], (TOKENS, C), 0.5, 3.0, ((0, 16), (1, 2))),
        "filter_raw": noise(splits[4], (L, F), 1.0, 4.0, ((0, 16), (1, 2))),
    }


def reference(x_one, x_two, values, grad_out, filter_raw):
    scale = 1.0 / math.sqrt(L)
    length = 2 * TOKENS
    blocks = C // F
    filt = filter_raw.astype(jnp.float32) * scale
    filt_spec = jnp.fft.rfft(filt, length, axis=0)
    product_in = (x_one.astype(jnp.float32) * values.astype(jnp.float32)).astype(jnp.bfloat16)
    grad_conv = (grad_out.astype(jnp.float32) * x_two.astype(jnp.float32)).astype(jnp.bfloat16)

    def arrange(array):
        return array.reshape(TOKENS, blocks, F).transpose(1, 0, 2)

    def per_block(items):
        prod_blk, grad_blk, out_blk, val_blk, one_blk = items
        prod_spec = jnp.fft.rfft(prod_blk.astype(jnp.float32), length, axis=0)
        grad_spec = jnp.fft.rfft(grad_blk.astype(jnp.float32), length, axis=0)
        conv_out = jnp.fft.irfft(prod_spec * filt_spec, length, axis=0)[:TOKENS]
        grad_in = jnp.fft.irfft(jnp.conj(filt_spec) * grad_spec, length, axis=0)[:TOKENS]
        corr = jnp.fft.irfft(jnp.conj(prod_spec) * grad_spec, length, axis=0)[:L]
        first = (grad_in * val_blk.astype(jnp.float32)).astype(jnp.bfloat16)
        second = (out_blk.astype(jnp.float32) * conv_out).astype(jnp.bfloat16)
        third = (grad_in * one_blk.astype(jnp.float32)).astype(jnp.bfloat16)
        return (first, second, third, corr)
    first, second, third, corr = lax.map(per_block, (arrange(product_in), arrange(grad_conv), arrange(grad_out), arrange(values), arrange(x_one)))

    def restore(array):
        return array.transpose(1, 0, 2).reshape(TOKENS, C)
    grad_filter = lax.optimization_barrier(jnp.sum(corr, axis=0)) * scale
    return (restore(first), restore(second), restore(third), grad_filter)
```

```python
import functools
import math

import jax
import jax.numpy as jnp
import ml_dtypes
import numpy as np
from jax import lax
from jax.experimental import pallas as pl
from jax.experimental.pallas import tpu as pltpu
from jax.sharding import PartitionSpec as P

GROUP = 4
f32 = jnp.float32
bf16 = jnp.bfloat16
VMEM_LIMIT = 48 * 1024 * 1024


def dft_tables(block):
    size = 2 * block
    place = np.arange(block)
    rows = []
    for parity in (0, 1):
        freq = np.arange(parity, block, 2)
        angle = 2.0 * math.pi / (2 * size) * ((2 * freq[:, None] + 1) * place[None, :] % (2 * size))
        rows += [np.cos(angle), -np.sin(angle)]
    table = np.concatenate(rows, axis=0)
    return table.astype(ml_dtypes.bfloat16), np.ascontiguousarray(table.T).astype(ml_dtypes.bfloat16)


def call(kernel, outs, *args, scratch=(), flops=0):
    bytes_accessed = sum(a.size * a.dtype.itemsize for a in args)
    bytes_accessed += sum(math.prod(s) * jnp.dtype(t).itemsize for s, t in outs)
    whole = pl.BlockSpec(memory_space=pltpu.VMEM)
    return pl.pallas_call(
        kernel,
        out_shape=[jax.ShapeDtypeStruct(s, t) for s, t in outs],
        in_specs=[whole] * len(args),
        out_specs=[whole] * len(outs),
        scratch_shapes=list(scratch),
        compiler_params=pltpu.CompilerParams(vmem_limit_bytes=VMEM_LIMIT),
        cost_estimate=pl.CostEstimate(flops=flops, bytes_accessed=bytes_accessed, transcendentals=0),
    )(*args)


def gate_kernel(groups, a_ref, b_ref, *outs):
    tok, chans = a_ref.shape
    part = groups // GROUP
    mine = lax.rem(lax.axis_index("ctx"), GROUP)
    for d in range(GROUP):
        for r in range(chans // groups):
            cols = pl.ds(pl.multiple_of(r * groups + (mine ^ d) * part, part), part)
            prod = a_ref[:, cols].astype(f32) * b_ref[:, cols].astype(f32)
            outs[d][:, r * part : (r + 1) * part] = prod.astype(bf16)


def assemble_kernel(*refs):
    out = refs[-1]
    rows = refs[0].shape[0]
    mine = lax.rem(lax.axis_index("ctx"), GROUP)
    for d in range(GROUP):
        out[pl.ds(pl.multiple_of((mine ^ d) * rows, rows), rows), :] = refs[d][...]


def filter_split_kernel(own_ref, peer_ref, *outs):
    part = outs[0].shape[1]
    mine = lax.rem(lax.axis_index("ctx"), GROUP)
    x = lax.axis_index("ch")
    for d in range(GROUP):
        to = mine ^ d
        cols = pl.ds(pl.multiple_of(lax.rem(to, 2) * part, part), part)

        @pl.when(to // 2 == x)
        def _():
            outs[d][...] = own_ref[:, cols]

        @pl.when(to // 2 != x)
        def _():
            outs[d][...] = peer_ref[:, cols]


def filter_spectra_kernel(scale, n_pieces, *refs):
    pieces, table_ref, out, taps_ref = refs[:n_pieces], refs[n_pieces], refs[n_pieces + 1], refs[n_pieces + 2]
    span, block, part = taps_ref.shape
    rows = pieces[0].shape[0]
    sup = lax.axis_index("ctx") // GROUP
    for d in range(n_pieces):
        at = (sup ^ d) * rows if n_pieces > 1 else 0
        if rows > block:
            for k in range(span):
                taps_ref[k] = pieces[d][k * block : (k + 1) * block, :]
        else:
            start = pl.multiple_of(lax.rem(at, block), rows)
            taps_ref[at // block, pl.ds(start, rows), :] = pieces[d][...]
    quarter = block // 2
    for k in range(span):
        spec = jnp.dot(table_ref[...], taps_ref[k], preferred_element_type=f32) * scale
        for parity, sign in ((0, 1.0), (1, -1.0)):
            re = slice(parity * block, parity * block + quarter)
            im = slice(parity * block + quarter, (parity + 1) * block)
            if k == 0:
                out[0, re, :] = spec[re]
                out[0, im, :] = spec[im]
            else:
                out[k, re, :] += spec[re]
                out[k, im, :] += spec[im]
            out[k + 1, re, :] = -sign * spec[im]
            out[k + 1, im, :] = sign * spec[re]


def conv_kernel(span, conj, with_lags, fast, scale, *refs):
    blocks = refs[: span + 1]
    at = span + 1
    if with_lags:
        own_grad = refs[at]
        at += 1
    weights, table, inverse = refs[at : at + 3]
    at += 3
    outs = refs[at : at + GROUP]
    at += GROUP
    n_lag = (2 if fast else 1) if with_lags else 0
    lag_outs = refs[at : at + n_lag]
    at += n_lag
    spec, prod, result = refs[at : at + 3]
    if with_lags:
        grad_spec, lag_prod, lag_result = refs[at + 3 : at + 6]
    block, wide = blocks[0].shape
    part = weights.shape[2]
    repeat = wide // part
    half = block // 2
    chunk = 32

    @pl.loop(0, 2)
    def _(parity):
        base = pl.multiple_of(parity * block, block)
        rows = table[pl.ds(base, block), :]
        for k in range(span + 1):
            spec[k] = jnp.dot(rows, blocks[k][...], preferred_element_type=f32)
        if with_lags:
            grad_spec[...] = jnp.dot(rows, own_grad[...], preferred_element_type=f32)
        sign = 1.0 - 2.0 * parity.astype(f32)

        @pl.loop(0, half // chunk)
        def _(step):
            lo = pl.multiple_of(step * chunk, chunk)
            re, im = pl.ds(lo, chunk), pl.ds(half + lo, chunk)
            re_at = pl.ds(pl.multiple_of(base + lo, chunk), chunk)
            im_at = pl.ds(pl.multiple_of(base + half + lo, chunk), chunk)
            lag = [None] * (span + 1)
            e_re = [weights[k, re_at, :] for k in range(span + 1)]
            e_im = [weights[k, im_at, :] for k in range(span + 1)]
            for r in range(repeat):
                cols = slice(r * part, (r + 1) * part)
                if with_lags:
                    g_re, g_im = grad_spec[re, cols], grad_spec[im, cols]
                y_re = y_im = None
                for k in range(span + 1):
                    a_re, a_im = spec[k, re, cols], spec[k, im, cols]
                    if conj:
                        t_re = e_re[k] * a_re + e_im[k] * a_im
                        t_im = e_re[k] * a_im - e_im[k] * a_re
                    else:
                        t_re = e_re[k] * a_re - e_im[k] * a_im
                        t_im = e_re[k] * a_im + e_im[k] * a_re
                    y_re = t_re if k == 0 else y_re + t_re
                    y_im = t_im if k == 0 else y_im + t_im
                    if with_lags:
                        c_re = g_re * a_re + g_im * a_im
                        c_im = g_im * a_re - g_re * a_im
                        lag[k] = (c_re, c_im) if r == 0 else (lag[k][0] + c_re, lag[k][1] + c_im)
                prod[re_at, cols] = y_re.astype(bf16)
                prod[im_at, cols] = y_im.astype(bf16)
            if with_lags:
                for k in range(span):
                    cols = slice(k * part, (k + 1) * part)
                    lag_prod[re_at, cols] = (lag[k][0] + sign * lag[k + 1][1]).astype(bf16)
                    lag_prod[im_at, cols] = (lag[k][1] - sign * lag[k + 1][0]).astype(bf16)

    result[...] = (jnp.dot(inverse[...], prod[...], preferred_element_type=f32) * (1.0 / block)).astype(bf16)
    rows = outs[0].shape[0]
    mine = lax.rem(lax.axis_index("ctx"), GROUP)
    for d in range(GROUP):
        outs[d][...] = result[pl.ds(pl.multiple_of((mine ^ d) * rows, rows), rows), :]
    if with_lags:
        lag_result[...] = jnp.dot(inverse[...], lag_prod[...], preferred_element_type=f32) * (scale / block)
        if fast:
            x = lax.axis_index("ch")
            keep, send = lag_outs
            piece = keep.shape[0] // (lax.axis_size("ctx") // GROUP)
            for s in range(keep.shape[0] // piece):
                k, low = divmod(2 * piece * s, block)
                cols = slice(k * part, (k + 1) * part)
                to = slice(s * piece, (s + 1) * piece)
                keep[to, :] = lag_result[pl.ds(pl.multiple_of(low + x * piece, piece), piece), cols]
                send[to, :] = lag_result[pl.ds(pl.multiple_of(low + (1 - x) * piece, piece), piece), cols]
        else:
            for k in range(span):
                lag_outs[0][k * block : (k + 1) * block, :] = lag_result[:, k * part : (k + 1) * part]


def lag_split_kernel(keep, recv, *outs):
    rows = outs[0].shape[0]
    sup = lax.axis_index("ctx") // GROUP
    for d in range(len(outs)):
        at = pl.ds(pl.multiple_of((sup ^ d) * rows, rows), rows)
        outs[d][...] = keep[at, :] + recv[at, :]


def lag_sum_kernel(n, *refs):
    terms, outs = refs[:n], refs[n : n + 2]
    rows = outs[0].shape[0]
    low = lax.rem(lax.axis_index("ctx"), 2)
    for p in range(2):
        at = pl.ds(pl.multiple_of((low ^ p) * rows, rows), rows)
        total = terms[0][at, :]
        for t in terms[1:]:
            total = total + t[at, :]
        outs[p][...] = total


def lag_place_kernel(a, b, out):
    part = a.shape[1]
    low = lax.rem(lax.axis_index("ctx"), 2)
    for p, ref in enumerate((a, b)):
        out[:, pl.ds(pl.multiple_of((low ^ p) * part, part), part)] = ref[...]


def finish_kernel(groups, n_gates, *refs):
    pieces, gates, outs = refs[:GROUP], refs[GROUP : GROUP + n_gates], refs[GROUP + n_gates :]
    part = groups // GROUP
    mine = lax.rem(lax.axis_index("ctx"), GROUP)
    for d in range(GROUP):
        for r in range(gates[0].shape[1] // groups):
            cols = pl.ds(pl.multiple_of(r * groups + (mine ^ d) * part, part), part)
            piece = pieces[d][:, r * part : (r + 1) * part].astype(f32)
            for gate, out in zip(gates, outs):
                out[:, cols] = (piece * gate[:, cols].astype(f32)).astype(bf16)


def local(x_one, x_two, values, grad_out, filter_raw):
    tok, chans = x_one.shape
    tap_rows, own_filters = filter_raw.shape
    n, n_ch = lax.axis_size("ctx"), lax.axis_size("ch")
    taps, groups = tap_rows * n, own_filters * n_ch
    part = groups // GROUP
    repeat = chans // groups
    wide = repeat * part
    block = GROUP * tok
    span = taps // block
    supers = n // GROUP
    scale = 1.0 / math.sqrt(taps)
    table_np, inverse_np = dft_tables(block)
    table, inverse = jnp.asarray(table_np), jnp.asarray(inverse_np)
    fast = n_ch == 2 and supers == 4 and taps // supers <= block

    def inside(value, d):
        return lax.ppermute(value, "ctx", [(i, i ^ d) for i in range(n)])

    def across(value, d):
        return lax.ppermute(value, "ctx", [(i, i ^ (d * GROUP)) for i in range(n)])

    def shift(value, by):
        by *= GROUP
        return lax.ppermute(value, "ctx", [(i, i + by) for i in range(n) if 0 <= i + by < n])

    def swap(value):
        return lax.ppermute(value, "ch", [(0, 1), (1, 0)])

    def trade(pieces):
        return [pieces[0]] + [inside(pieces[d], d) for d in range(1, GROUP)]

    def gated(a, b):
        pieces = call(functools.partial(gate_kernel, groups), [((tok, wide), bf16)] * GROUP, a, b)
        return call(assemble_kernel, [((block, wide), bf16)], *trade(pieces))[0]

    def hops(own, by):
        blocks = [own]
        for _ in range(span):
            blocks.append(shift(blocks[-1], by))
        return blocks

    if fast:
        peer = swap(filter_raw)
        pieces = call(filter_split_kernel, [((tap_rows, part), bf16)] * GROUP, filter_raw, peer)
        rows = call(assemble_kernel, [((GROUP * tap_rows, part), bf16)], *trade(pieces))[0]
        filt = [rows] + [across(rows, d) for d in range(1, supers)]
    else:
        whole = lax.all_gather(filter_raw, "ctx", axis=0, tiled=True)
        whole = lax.all_gather(whole, "ch", axis=1, tiled=True)
        start = lax.rem(lax.axis_index("ctx"), GROUP) * part
        filt = [lax.dynamic_slice(whole, (0, start), (taps, part))]
    p_blocks = hops(gated(x_one, values), 1)
    g_blocks = hops(gated(grad_out, x_two), -1)
    weights = call(
        functools.partial(filter_spectra_kernel, scale, len(filt)),
        [((span + 1, 2 * block, part), f32)],
        *filt,
        table,
        scratch=[pltpu.VMEM((span, block, part), bf16)],
        flops=4 * block * block * part * span,
    )[0]

    work = [
        pltpu.VMEM((span + 1, block, wide), f32),
        pltpu.VMEM((2 * block, wide), bf16),
        pltpu.VMEM((block, wide), bf16),
    ]
    lag_work = [
        pltpu.VMEM((block, wide), f32),
        pltpu.VMEM((2 * block, span * part), bf16),
        pltpu.VMEM((block, span * part), f32),
    ]
    lag_shapes = [((taps // 2, part), f32)] * 2 if fast else [((taps, part), f32)]
    made = call(
        functools.partial(conv_kernel, span, False, True, fast, scale),
        [((tok, wide), bf16)] * GROUP + lag_shapes,
        *p_blocks,
        g_blocks[0],
        weights,
        table,
        inverse,
        scratch=work + lag_work,
        flops=4 * block * block * wide * (span + 3),
    )
    conv, lags = trade(made[:GROUP]), made[GROUP:]
    back = call(
        functools.partial(conv_kernel, span, True, False, fast, scale),
        [((tok, wide), bf16)] * GROUP,
        *g_blocks,
        weights,
        table,
        inverse,
        scratch=work,
        flops=4 * block * block * wide * (span + 2),
    )
    grad_in = trade(back)
    gate_shape = ((tok, chans), bf16)
    grad_x_two = call(functools.partial(finish_kernel, groups, 1), [gate_shape], *conv, grad_out)[0]
    grad_x_one, grad_values = call(
        functools.partial(finish_kernel, groups, 2), [gate_shape] * 2, *grad_in, values, x_one
    )

    if fast:
        keep, send = lags
        rows = taps // 2 // supers
        pieces = call(lag_split_kernel, [((rows, part), f32)] * supers, keep, swap(send))
        terms = [pieces[0]] + [across(pieces[d], d) for d in range(1, supers)]
        sums = call(functools.partial(lag_sum_kernel, supers), [((tap_rows, part), f32)] * 2, *terms)

        def owner(value, p):
            pairs = []
            for i in range(n):
                j1, j0 = (i // 2) % 2, i % 2
                for x in range(2):
                    to = i // GROUP * GROUP + 2 * x + (p ^ j0)
                    pairs.append((i * 2 + x, to * 2 + j1))
            return lax.ppermute(value, ("ctx", "ch"), pairs)

        landed = [owner(s, p) for p, s in enumerate(sums)]
        grad_filter = call(lag_place_kernel, [((tap_rows, own_filters), f32)], *landed)[0]
    else:
        start = lax.rem(lax.axis_index("ctx"), GROUP) * part
        terms = lax.dynamic_update_slice(jnp.zeros((taps, groups), f32), lags[0], (0, start))
        by_taps = lax.psum_scatter(terms, "ctx", scatter_dimension=0, tiled=True)
        grad_filter = lax.psum_scatter(by_taps, "ch", scatter_dimension=1, tiled=True)
    return (grad_x_one, grad_x_two, grad_values, grad_filter)


def solution(mesh):
    placed = P("ctx", "ch")
    return jax.shard_map(
        local,
        mesh=mesh,
        in_specs=(placed,) * 5,
        out_specs=(placed,) * 4,
        check_vma=False,
    )
```

```python
import functools
import math

import jax
import jax.numpy as jnp
import ml_dtypes
import numpy as np
from jax import lax
from jax.experimental import pallas as pl
from jax.experimental.pallas import tpu as pltpu
from jax.sharding import PartitionSpec as P

GROUP = 4
f32 = jnp.float32
bf16 = jnp.bfloat16
VMEM_LIMIT = 24 * 1024 * 1024
BINS = 16


def dft_tables(block):
    size = 2 * block
    place = np.arange(block)
    rows = []
    for parity in (0, 1):
        freq = np.arange(parity, block, 2)
        angle = 2.0 * math.pi / (2 * size) * ((2 * freq[:, None] + 1) * place[None, :] % (2 * size))
        rows += [np.cos(angle), -np.sin(angle)]
    table = np.concatenate(rows, axis=0)
    high = table.astype(ml_dtypes.bfloat16)
    rest = (table - high.astype(np.float64)).astype(ml_dtypes.bfloat16)
    return high, rest, np.ascontiguousarray(high.T), np.ascontiguousarray(rest.T)


def call(kernel, outs, *args, scratch=(), flops=0, specs=None, out_specs=None, after=()):
    bytes_accessed = sum(a.size * a.dtype.itemsize for a in args)
    bytes_accessed += sum(math.prod(s) * jnp.dtype(t).itemsize for s, t in outs)
    whole = pl.BlockSpec(memory_space=pltpu.VMEM)
    n_args, n_after = len(args), len(after)

    def run(*refs):
        kernel(*refs[:n_args], *refs[n_args + n_after :])

    return pl.pallas_call(
        run,
        out_shape=[jax.ShapeDtypeStruct(s, t) for s, t in outs],
        in_specs=(specs or [whole] * n_args) + [pl.BlockSpec(memory_space=pl.ANY)] * n_after,
        out_specs=out_specs or [whole] * len(outs),
        scratch_shapes=list(scratch),
        compiler_params=pltpu.CompilerParams(vmem_limit_bytes=VMEM_LIMIT),
        cost_estimate=pl.CostEstimate(flops=0, bytes_accessed=0, transcendentals=0),
    )(*args, *after)


def gate_kernel(groups, chunks, *refs):
    hbm, outs, bufs, sems = refs[:4], refs[4 : 4 + GROUP], refs[4 + GROUP : 8 + GROUP], refs[8 + GROUP]
    tok, chans = bufs[0].shape
    part = groups // GROUP
    mine = lax.rem(lax.axis_index("ctx"), GROUP)
    step = tok // chunks
    copies = []
    for s in (0, 2):
        for i in range(chunks):
            rows = pl.ds(i * step, step)
            copies.append(
                [pltpu.make_async_copy(hbm[a].at[rows], bufs[a].at[rows], sems.at[a, i]) for a in (s, s + 1)]
            )
            for copy in copies[-1]:
                copy.start()
    for s in range(2):
        for i in range(chunks):
            for copy in copies[s * chunks + i]:
                copy.wait()
            rows, to = slice(i * step, (i + 1) * step), slice(s * tok + i * step, s * tok + (i + 1) * step)
            for d in range(GROUP):
                for r in range(chans // groups):
                    at = pl.ds(pl.multiple_of(r * groups + (mine ^ d) * part, part), part)
                    prod = bufs[2 * s][rows, at].astype(f32) * bufs[2 * s + 1][rows, at].astype(f32)
                    outs[d][to, r * part : (r + 1) * part] = prod.astype(bf16)


def assemble(pieces, p_out, g_out):
    rows = p_out.shape[0] // GROUP
    mine = lax.rem(lax.axis_index("ctx"), GROUP)
    for d in range(GROUP):
        at = pl.ds(pl.multiple_of((mine ^ d) * rows, rows), rows)
        p_out[at, :] = pieces[d][:rows, :]
        g_out[at, :] = pieces[d][rows:, :]


def assemble_kernel(*refs):
    assemble(refs[:GROUP], *refs[GROUP:])


def join_kernel(own, peer, out):
    part = own.shape[1]
    x = lax.axis_index("ch")
    for at, ref in ((x, own), (1 - x, peer)):
        out[:, pl.ds(pl.multiple_of(at * part, part), part)] = ref[...]


def assemble_split_kernel(*refs):
    pieces, raw, outs = refs[:GROUP], refs[GROUP : -GROUP - 2], refs[-GROUP:]
    assemble(pieces, *refs[-GROUP - 2 : -GROUP])
    part = outs[0].shape[1]
    sup, mine = lax.axis_index("ctx") // GROUP, lax.rem(lax.axis_index("ctx"), GROUP)
    for i, ref in enumerate(raw):
        rows = ref.shape[0]
        at = pl.ds(pl.multiple_of((sup ^ i) * rows, rows), rows)
        for d in range(GROUP):
            outs[d][at, :] = ref[:, pl.ds(pl.multiple_of((mine ^ d) * part, part), part)]


def pass_kernel(value, out):
    out[...] = value[...]


def filter_spectra_kernel(scale, fast, *refs):
    table_ref, rest_ref, out, taps_ref = refs[-4:]
    pieces = refs[:-4]
    n_slabs, slab, part = taps_ref.shape
    block = table_ref.shape[1]
    mine = lax.rem(lax.axis_index("ctx"), GROUP)
    for s in range(n_slabs):
        if fast:
            rows = slab // GROUP
            for d in range(GROUP):
                at = pl.ds(pl.multiple_of((mine ^ d) * rows, rows), rows)
                taps_ref[s, at, :] = pieces[d][s * rows : (s + 1) * rows, :]
        else:
            taps_ref[s] = pieces[0][s * slab : (s + 1) * slab, :]
    quarter = block // 2
    each = block // slab
    for k in range(n_slabs // each):
        spec = None
        for i in range(each):
            cols = slice(i * slab, (i + 1) * slab)
            for t in (table_ref, rest_ref):
                term = jnp.dot(t[:, cols], taps_ref[k * each + i], preferred_element_type=f32)
                spec = term if spec is None else spec + term
        spec = spec * scale
        for parity, sign in ((0, 1.0), (1, -1.0)):
            re = slice(parity * block, parity * block + quarter)
            im = slice(parity * block + quarter, (parity + 1) * block)
            if k == 0:
                out[0, re, :] = spec[re]
                out[0, im, :] = spec[im]
            else:
                out[k, re, :] += spec[re]
                out[k, im, :] += spec[im]
            out[k + 1, re, :] = -sign * spec[im]
            out[k + 1, im, :] = sign * spec[re]


def times(e_re, e_im, a_re, a_im, conj):
    if conj:
        return e_re * a_re + e_im * a_im, e_re * a_im - e_im * a_re
    return e_re * a_re - e_im * a_im, e_re * a_im + e_im * a_re


def bin_rows(block, visit):
    @pl.loop(0, 2)
    def _(parity):
        sign = 1.0 - 2.0 * parity.astype(f32)

        @pl.loop(0, block // 2 // BINS)
        def _(step):
            re = pl.multiple_of(parity * block + step * BINS, BINS)
            im = pl.multiple_of(parity * block + block // 2 + step * BINS, BINS)
            visit(sign, pl.ds(re, BINS), pl.ds(im, BINS))


def lag_kernel(fast, scale, *refs):
    blocks, (table, inverse, inverse_rest), refs = refs[:4], refs[4:7], refs[7:]
    spec, refs = refs[0], refs[1:]
    n_out = 2 if fast else 1
    lag_outs, (lag_prod, lag_low, lag_result) = refs[:n_out], refs[n_out:]
    block, wide = blocks[0].shape
    part = lag_result.shape[1] // 2
    for i, ref in enumerate(blocks):
        spec[i] = jnp.dot(table[...], ref[...], preferred_element_type=f32)

    def visit(sign, re, im):
        lags = [None] * 3
        for r in range(wide // part):
            cols = slice(r * part, (r + 1) * part)
            p0, p1, g0, g1 = ((spec[i, re, cols], spec[i, im, cols]) for i in range(4))
            for k, (p, g) in enumerate(((p0, g0), (p1, g0), (p1, g1))):
                t = times(*p, *g, True)
                lags[k] = t if lags[k] is None else (lags[k][0] + t[0], lags[k][1] + t[1])
        for k in range(2):
            cols = slice(k * part, (k + 1) * part)
            w_re = lags[k][0] + sign * lags[k + 1][1]
            w_im = lags[k][1] - sign * lags[k + 1][0]
            for rows, w in ((re, w_re), (im, w_im)):
                high = w.astype(bf16)
                lag_prod[rows, cols] = high
                lag_low[rows, cols] = (w - high.astype(f32)).astype(bf16)

    bin_rows(block, visit)
    total = jnp.dot(inverse[...], lag_prod[...], preferred_element_type=f32)
    total = total + jnp.dot(inverse[...], lag_low[...], preferred_element_type=f32)
    total = total + jnp.dot(inverse_rest[...], lag_prod[...], preferred_element_type=f32)
    lag_result[...] = total * (scale / block)
    if fast:
        x = lax.axis_index("ch")
        keep, send = lag_outs
        piece = keep.shape[0] // (lax.axis_size("ctx") // GROUP)
        for s in range(keep.shape[0] // piece):
            i, low = divmod(2 * piece * s, block)
            cols = slice(i * part, (i + 1) * part)
            to = slice(s * piece, (s + 1) * piece)
            keep[to, :] = lag_result[pl.ds(pl.multiple_of(low + x * piece, piece), piece), cols]
            send[to, :] = lag_result[pl.ds(pl.multiple_of(low + (1 - x) * piece, piece), piece), cols]
    else:
        for i in range(2):
            lag_outs[0][i * block : (i + 1) * block, :] = lag_result[:, i * part : (i + 1) * part]


def conv_kernel(conj, far, near, weights, table, inverse, *refs):
    outs, (spec, prod, result) = refs[:GROUP], refs[GROUP:]
    block, wide = far.shape
    part = weights.shape[2]
    first = 2 if conj else 0
    spec[...] = jnp.dot(table[...], far[...], preferred_element_type=f32)

    def visit(sign, re, im):
        e = [(weights[k, re, :], weights[k, im, :]) for k in range(3)]
        for r in range(wide // part):
            cols = slice(r * part, (r + 1) * part)
            total = times(*e[2], spec[re, cols], spec[im, cols], conj)
            for k in range(2):
                t = times(*e[k], near[first + k, re, cols], near[first + k, im, cols], conj)
                total = total[0] + t[0], total[1] + t[1]
            prod[re, cols] = total[0].astype(bf16)
            prod[im, cols] = total[1].astype(bf16)

    bin_rows(block, visit)
    result[...] = (jnp.dot(inverse[...], prod[...], preferred_element_type=f32) * (1.0 / block)).astype(bf16)
    rows = outs[0].shape[0]
    mine = lax.rem(lax.axis_index("ctx"), GROUP)
    for d in range(GROUP):
        outs[d][...] = result[pl.ds(pl.multiple_of((mine ^ d) * rows, rows), rows), :]


def lag_half_kernel(by, a, b, mine, theirs):
    rows = mine.shape[0]
    side = lax.rem(lax.axis_index("ctx") // (GROUP * by), 2)
    for out, at in ((mine, side), (theirs, 1 - side)):
        at = pl.ds(pl.multiple_of(at * rows, rows), rows)
        out[...] = a[at, :] + b[at, :]


def lag_sum_kernel(a, b, *outs):
    rows = outs[0].shape[0]
    low = lax.rem(lax.axis_index("ctx"), 2)
    for p in range(2):
        at = pl.ds(pl.multiple_of((low ^ p) * rows, rows), rows)
        outs[p][...] = a[at, :] + b[at, :]


def lag_place_kernel(a, b, out):
    part = a.shape[1]
    low = lax.rem(lax.axis_index("ctx"), 2)
    for p, ref in enumerate((a, b)):
        out[:, pl.ds(pl.multiple_of((low ^ p) * part, part), part)] = ref[...]


def finish_kernel(groups, chunks, n, *refs):
    pieces, gates, refs = refs[:GROUP], refs[GROUP : GROUP + n], refs[GROUP + n :]
    hbm, token, bufs, sems = refs[:n], refs[n], refs[n + 1 : 2 * n + 1], refs[2 * n + 1]
    tok, chans = gates[0].shape
    part = groups // GROUP
    mine = lax.rem(lax.axis_index("ctx"), GROUP)
    step = tok // chunks
    copies = []
    for i in range(chunks):
        rows = slice(i * step, (i + 1) * step)
        for d in range(GROUP):
            for r in range(chans // groups):
                cols = pl.ds(pl.multiple_of(r * groups + (mine ^ d) * part, part), part)
                piece = pieces[d][rows, r * part : (r + 1) * part].astype(f32)
                for a in range(n):
                    bufs[a][rows, cols] = (piece * gates[a][rows, cols].astype(f32)).astype(bf16)
        for a in range(n):
            at = pl.ds(i * step, step)
            copies.append(pltpu.make_async_copy(bufs[a].at[at], hbm[a].at[at], sems.at[a, i]))
            copies[-1].start()
    token[...] = jnp.zeros_like(token)
    for copy in copies:
        copy.wait()


def local(x_one, x_two, values, grad_out, filter_raw):
    tok, chans = x_one.shape
    tap_rows, own_filters = filter_raw.shape
    n, n_ch = lax.axis_size("ctx"), lax.axis_size("ch")
    taps, groups = tap_rows * n, own_filters * n_ch
    part = groups // GROUP
    repeat = chans // groups
    wide = repeat * part
    block = GROUP * tok
    span = taps // block
    assert span == 2 and taps % block == 0
    supers = n // GROUP
    scale = 1.0 / math.sqrt(taps)
    table, rest, inverse, inverse_rest = (jnp.asarray(t) for t in dft_tables(block))
    fast = n_ch == 2 and supers == 4 and taps // supers <= block

    def inside(value, d):
        return lax.ppermute(value, "ctx", [(i, i ^ d) for i in range(n)])

    def across(value, d):
        return lax.ppermute(value, "ctx", [(i, i ^ (d * GROUP)) for i in range(n)])

    def shift(value, by):
        by *= GROUP
        return lax.ppermute(value, "ctx", [(i, i + by) for i in range(n) if 0 <= i + by < n])

    def swap(value):
        return lax.ppermute(value, "ch", [(0, 1), (1, 0)])

    def trade(pieces):
        return [pieces[0]] + [inside(pieces[d], d) for d in range(1, GROUP)]

    chunks = 4
    in_hbm, in_vmem = pl.BlockSpec(memory_space=pltpu.HBM), pl.BlockSpec(memory_space=pltpu.VMEM)
    pieces_shape = [((tok, wide), bf16)] * GROUP
    block_shape = ((block, wide), bf16)

    gates = call(
        functools.partial(gate_kernel, groups, chunks),
        [((2 * tok, wide), bf16)] * GROUP,
        *(pltpu.with_memory_space_constraint(a, pltpu.HBM) for a in (x_one, values, grad_out, x_two)),
        scratch=[pltpu.VMEM((tok, chans), bf16)] * 4 + [pltpu.SemaphoreType.DMA((4, chunks))],
        specs=[in_hbm] * 4,
    )
    pieces = trade(gates)
    if fast:
        own_rows = call(join_kernel, [((tap_rows, groups), bf16)], filter_raw, swap(filter_raw), after=[pieces[1]])[0]
        raw = [own_rows] + [across(own_rows, d) for d in range(1, supers)]
        p_own, g_own, *filt = call(
            assemble_split_kernel,
            [block_shape, block_shape] + [((supers * tap_rows, part), bf16)] * GROUP,
            *pieces,
            *raw,
        )
        filt = trade(filt)
    else:
        p_own, g_own = call(assemble_kernel, [block_shape, block_shape], *pieces)
        whole = lax.all_gather(filter_raw, "ctx", axis=0, tiled=True)
        whole = lax.all_gather(whole, "ch", axis=1, tiled=True)
        start = lax.rem(lax.axis_index("ctx"), GROUP) * part
        filt = [lax.dynamic_slice(whole, (0, start), (taps, part))]
    slab = taps // supers if fast else block
    weights = call(
        functools.partial(filter_spectra_kernel, scale, fast),
        [((3, 2 * block, part), f32)],
        *filt,
        table,
        rest,
        scratch=[pltpu.VMEM((taps // slab, slab, part), bf16)],
    )[0]
    p_back, g_ahead = shift(p_own, 1), shift(g_own, -1)
    p_next = call(pass_kernel, [block_shape], p_back, after=[weights])[0]
    p_far, g_far = shift(p_next, 1), shift(g_ahead, -1)
    near, *lags = call(
        functools.partial(lag_kernel, fast, scale),
        [((4, 2 * block, wide), f32)] + ([((taps // 2, part), f32)] * 2 if fast else [((taps, part), f32)]),
        p_own,
        p_back,
        g_own,
        g_ahead,
        table,
        inverse,
        inverse_rest,
        scratch=[pltpu.VMEM((2 * block, 2 * part), bf16)] * 2
        + [pltpu.VMEM((block, 2 * part), f32)],
        after=[weights],
    )

    def convolve(conj, prior, far, *more):
        return call(
            functools.partial(conv_kernel, conj),
            pieces_shape,
            far,
            near,
            weights,
            table,
            inverse,
            scratch=[
                pltpu.VMEM((2 * block, wide), f32),
                pltpu.VMEM((2 * block, wide), bf16),
                pltpu.VMEM((block, wide), bf16),
            ],
            after=[prior, *more],
        )

    def finish(pieces, prior, *gates):
        n = len(gates)
        return call(
            functools.partial(finish_kernel, groups, chunks, n),
            [((tok, chans), bf16)] * n + [((8, 128), f32)],
            *pieces,
            *gates,
            scratch=[pltpu.VMEM((tok, chans), bf16)] * n + [pltpu.SemaphoreType.DMA((n, chunks))],
            out_specs=[in_hbm] * n + [in_vmem],
            after=[prior],
        )

    conv = convolve(False, lags[0], p_far)
    prior = conv[0]
    if fast:
        mine, theirs = lags
        mine, theirs = call(
            functools.partial(lag_half_kernel, 2),
            [((taps // 4, part), f32)] * 2,
            mine,
            swap(theirs),
            after=[prior],
        )
        prior = mine
    conv = trade(conv)
    back = convolve(True, prior, g_far, conv[1])
    prior = back[0]
    if fast:
        mine, theirs = call(
            functools.partial(lag_half_kernel, 1),
            [((taps // 8, part), f32)] * 2,
            mine,
            across(theirs, 2),
            after=[prior],
        )
        prior = mine
    grad_x_two, prior = finish(conv, prior, grad_out)
    if fast:
        sums = call(
            lag_sum_kernel, [((tap_rows, part), f32)] * 2, mine, across(theirs, 1), after=[prior]
        )
        prior = sums[0]
    grad_x_one, grad_values, prior = finish(trade(back), prior, values, x_one)
    if fast:

        def owner(value, p):
            pairs = []
            for i in range(n):
                j1, j0 = (i // 2) % 2, i % 2
                for x in range(2):
                    to = i // GROUP * GROUP + 2 * x + (p ^ j0)
                    pairs.append((i * 2 + x, to * 2 + j1))
            return lax.ppermute(value, ("ctx", "ch"), pairs)

        landed = [owner(s, p) for p, s in enumerate(sums)]
        grad_filter = call(lag_place_kernel, [((tap_rows, own_filters), f32)], *landed, after=[prior])[0]
    else:
        start = lax.rem(lax.axis_index("ctx"), GROUP) * part
        terms = lax.dynamic_update_slice(jnp.zeros((taps, groups), f32), lags[0], (0, start))
        by_taps = lax.psum_scatter(terms, "ctx", scatter_dimension=0, tiled=True)
        grad_filter = lax.psum_scatter(by_taps, "ch", scatter_dimension=1, tiled=True)
    return (grad_x_one, grad_x_two, grad_values, grad_filter)


def solution(mesh):
    placed = P("ctx", "ch")
    return jax.shard_map(
        local,
        mesh=mesh,
        in_specs=(placed,) * 5,
        out_specs=(placed,) * 4,
        check_vma=False,
    )
```

```python
import functools
import math

import jax
import jax.numpy as jnp
import ml_dtypes
import numpy as np
from jax import lax
from jax.experimental import pallas as pl
from jax.experimental.pallas import tpu as pltpu
from jax.sharding import PartitionSpec as P

GROUP = 4
f32 = jnp.float32
bf16 = jnp.bfloat16
VMEM_LIMIT = 24 * 1024 * 1024
BINS = 16


def dft_tables(block):
    size = 2 * block
    place = np.arange(block)
    rows = []
    for parity in (0, 1):
        freq = np.arange(parity, block, 2)
        angle = 2.0 * math.pi / (2 * size) * ((2 * freq[:, None] + 1) * place[None, :] % (2 * size))
        rows += [np.cos(angle), -np.sin(angle)]
    table = np.concatenate(rows, axis=0)
    high = table.astype(ml_dtypes.bfloat16)
    rest = (table - high.astype(np.float64)).astype(ml_dtypes.bfloat16)
    return high, rest, np.ascontiguousarray(high.T), np.ascontiguousarray(rest.T)


def call(kernel, outs, *args, scratch=(), flops=0, specs=None, out_specs=None, after=(), aliases=None):
    bytes_accessed = sum(a.size * a.dtype.itemsize for a in args)
    bytes_accessed += sum(math.prod(s) * jnp.dtype(t).itemsize for s, t in outs)
    whole = pl.BlockSpec(memory_space=pltpu.VMEM)
    n_args, n_after = len(args), len(after)

    def run(*refs):
        kernel(*refs[:n_args], *refs[n_args + n_after :])

    return pl.pallas_call(
        run,
        out_shape=[jax.ShapeDtypeStruct(s, t) for s, t in outs],
        in_specs=(specs or [whole] * n_args) + [pl.BlockSpec(memory_space=pl.ANY)] * n_after,
        out_specs=out_specs or [whole] * len(outs),
        scratch_shapes=list(scratch),
        input_output_aliases=aliases or {},
        compiler_params=pltpu.CompilerParams(vmem_limit_bytes=VMEM_LIMIT),
        cost_estimate=pl.CostEstimate(flops=0, bytes_accessed=0, transcendentals=0),
    )(*args, *after)


def gate_kernel(groups, chunks, *refs):
    hbm, outs, bufs, sems = refs[:4], refs[4 : 4 + GROUP], refs[4 + GROUP : 8 + GROUP], refs[8 + GROUP]
    tok, chans = bufs[0].shape
    part = groups // GROUP
    mine = lax.rem(lax.axis_index("ctx"), GROUP)
    step = tok // chunks
    copies = []
    for s in (0, 2):
        for i in range(chunks):
            rows = pl.ds(i * step, step)
            copies.append(
                [pltpu.make_async_copy(hbm[a].at[rows], bufs[a].at[rows], sems.at[a, i]) for a in (s, s + 1)]
            )
            for copy in copies[-1]:
                copy.start()
    for s in range(2):
        for i in range(chunks):
            for copy in copies[s * chunks + i]:
                copy.wait()
            rows, to = slice(i * step, (i + 1) * step), slice(s * tok + i * step, s * tok + (i + 1) * step)
            for d in range(GROUP):
                for r in range(chans // groups):
                    at = pl.ds(pl.multiple_of(r * groups + (mine ^ d) * part, part), part)
                    prod = bufs[2 * s][rows, at].astype(f32) * bufs[2 * s + 1][rows, at].astype(f32)
                    outs[d][to, r * part : (r + 1) * part] = prod.astype(bf16)


def even_super():
    return lax.rem(lax.axis_index("ctx") // GROUP, 2) == 0


def assemble(pieces, lower, upper):
    rows = lower.shape[0] // GROUP
    mine = lax.rem(lax.axis_index("ctx"), GROUP)

    def place(p_out, g_out):
        for d in range(GROUP):
            at = pl.ds(pl.multiple_of((mine ^ d) * rows, rows), rows)
            p_out[at, :] = pieces[d][:rows, :]
            g_out[at, :] = pieces[d][rows:, :]

    even = even_super()
    pl.when(even)(lambda: place(lower, upper))
    pl.when(jnp.logical_not(even))(lambda: place(upper, lower))


def assemble_kernel(*refs):
    assemble(refs[:GROUP], *refs[GROUP:])


def assemble_split_kernel(*refs):
    pieces, raw, (lower, upper, *outs) = refs[:GROUP], refs[GROUP:-4], refs[-4:]
    assemble(pieces, lower, upper)
    sup, low = lax.axis_index("ctx") // GROUP, lax.rem(lax.axis_index("ctx"), 2)
    rows, part = raw[0].shape[0], outs[0].shape[1]
    for d, ref in enumerate(raw):
        at = pl.ds(pl.multiple_of((sup ^ d) * rows, rows), rows)
        for p in range(2):
            outs[p][at, :] = ref[:, pl.ds(pl.multiple_of((low ^ p) * part, part), part)]


def pass_kernel(value, out):
    out[...] = value[...]


def filter_spectra_kernel(scale, fast, *refs):
    table_ref, rest_ref, out, taps_ref = refs[-4:]
    pieces = refs[:-4]
    n_slabs, slab, part = taps_ref.shape
    block = table_ref.shape[1]
    mine = lax.rem(lax.axis_index("ctx"), GROUP)
    for s in range(n_slabs):
        if fast:
            rows = slab // GROUP
            for d in range(GROUP):
                p, q = divmod(d, 2)
                member = (q ^ lax.axis_index("ch")) * 2 + (p ^ lax.rem(mine, 2))
                at = pl.ds(pl.multiple_of(member * rows, rows), rows)
                taps_ref[s, at, :] = pieces[d][s * rows : (s + 1) * rows, :]
        else:
            taps_ref[s] = pieces[0][s * slab : (s + 1) * slab, :]
    quarter = block // 2
    each = block // slab
    for k in range(n_slabs // each):
        spec = None
        for i in range(each):
            cols = slice(i * slab, (i + 1) * slab)
            for t in (table_ref, rest_ref):
                term = jnp.dot(t[:, cols], taps_ref[k * each + i], preferred_element_type=f32)
                spec = term if spec is None else spec + term
        spec = spec * scale
        for parity, sign in ((0, 1.0), (1, -1.0)):
            re = slice(parity * block, parity * block + quarter)
            im = slice(parity * block + quarter, (parity + 1) * block)
            if k == 0:
                out[0, re, :] = spec[re]
                out[0, im, :] = spec[im]
            else:
                out[k, re, :] += spec[re]
                out[k, im, :] += spec[im]
            out[k + 1, re, :] = -sign * spec[im]
            out[k + 1, im, :] = sign * spec[re]


def times(e_re, e_im, a_re, a_im):
    return e_re * a_re - e_im * a_im, e_re * a_im + e_im * a_re


def conj_times(e_re, e_im, a_re, a_im):
    return e_re * a_re + e_im * a_im, e_re * a_im - e_im * a_re


def bin_rows(block, visit):
    @pl.loop(0, 2)
    def _(parity):
        sign = 1.0 - 2.0 * parity.astype(f32)

        @pl.loop(0, block // 2 // BINS)
        def _(step):
            re = pl.multiple_of(parity * block + step * BINS, BINS)
            im = pl.multiple_of(parity * block + block // 2 + step * BINS, BINS)
            visit(sign, pl.ds(re, BINS), pl.ds(im, BINS))


def own_kernel(lower, upper, table, spec, lag):
    block, wide = lower.shape
    part = lag.shape[1]
    spec[0] = jnp.dot(table[...], lower[...], preferred_element_type=f32)
    spec[1] = jnp.dot(table[...], upper[...], preferred_element_type=f32)
    sign = jnp.where(even_super(), 1.0, -1.0).astype(f32)

    def visit(_, re, im):
        total = None
        for r in range(wide // part):
            cols = slice(r * part, (r + 1) * part)
            t = conj_times(spec[0, re, cols], spec[0, im, cols], spec[1, re, cols], spec[1, im, cols])
            total = t if total is None else (total[0] + t[0], total[1] + t[1])
        lag[re, :], lag[im, :] = total[0], total[1] * sign

    bin_rows(block, visit)


def lag_kernel(fast, scale, one, two, own, own_lag, table, inverse, inverse_rest, spec, *refs):
    n_out = 2 if fast else 1
    lag_outs, (lag_prod, lag_low, lag_result) = refs[:n_out], refs[n_out:]
    block, wide = one.shape
    part = own_lag.shape[1]
    spec[0] = jnp.dot(table[...], one[...], preferred_element_type=f32)
    spec[1] = jnp.dot(table[...], two[...], preferred_element_type=f32)
    at = jnp.where(even_super(), 1, 0)

    def visit(sign, re, im):
        lags = [(own_lag[re, :], own_lag[im, :]), None, None]
        for r in range(wide // part):
            cols = slice(r * part, (r + 1) * part)
            p1 = spec[at, re, cols], spec[at, im, cols]
            g1 = spec[1 - at, re, cols], spec[1 - at, im, cols]
            g0 = own[at, re, cols], own[at, im, cols]
            for k, (p, g) in ((1, (p1, g0)), (2, (p1, g1))):
                t = conj_times(*p, *g)
                lags[k] = t if lags[k] is None else (lags[k][0] + t[0], lags[k][1] + t[1])
        for k in range(2):
            cols = slice(k * part, (k + 1) * part)
            w_re = lags[k][0] + sign * lags[k + 1][1]
            w_im = lags[k][1] - sign * lags[k + 1][0]
            for rows, w in ((re, w_re), (im, w_im)):
                high = w.astype(bf16)
                lag_prod[rows, cols] = high
                lag_low[rows, cols] = (w - high.astype(f32)).astype(bf16)

    bin_rows(block, visit)
    total = jnp.dot(inverse[...], lag_prod[...], preferred_element_type=f32)
    total = total + jnp.dot(inverse[...], lag_low[...], preferred_element_type=f32)
    total = total + jnp.dot(inverse_rest[...], lag_prod[...], preferred_element_type=f32)
    lag_result[...] = total * (scale / block)
    if fast:
        x = lax.axis_index("ch")
        keep, send = lag_outs
        piece = keep.shape[0] // (lax.axis_size("ctx") // GROUP)
        for s in range(keep.shape[0] // piece):
            i, low = divmod(2 * piece * s, block)
            cols = slice(i * part, (i + 1) * part)
            to = slice(s * piece, (s + 1) * piece)
            keep[to, :] = lag_result[pl.ds(pl.multiple_of(low + x * piece, piece), piece), cols]
            there = pl.ds(pl.multiple_of(low + (1 - x) * piece, piece), piece)
            send[to, :] = lag_result[there, cols].astype(bf16)
    else:
        for i in range(2):
            lag_outs[0][i * block : (i + 1) * block, :] = lag_result[:, i * part : (i + 1) * part]


def conv_kernel(which, far, near, own, weights, table, inverse, *refs):
    outs, (spec, prod, result) = refs[:GROUP], refs[GROUP:]
    block, wide = far.shape
    part = weights.shape[2]
    conj = jnp.where(even_super(), 1 - which, which)
    side = (1 - 2 * conj).astype(f32)
    spec[...] = jnp.dot(table[...], far[...], preferred_element_type=f32)

    def visit(_, re, im):
        e = [(weights[k, re, :], weights[k, im, :] * side) for k in range(3)]
        for r in range(wide // part):
            cols = slice(r * part, (r + 1) * part)
            total = times(*e[2], spec[re, cols], spec[im, cols])
            for k, ref, i in ((0, own, 1 - which), (1, near, which)):
                t = times(*e[k], ref[i, re, cols], ref[i, im, cols])
                total = total[0] + t[0], total[1] + t[1]
            prod[re, cols] = total[0].astype(bf16)
            prod[im, cols] = total[1].astype(bf16)

    bin_rows(block, visit)
    result[...] = (jnp.dot(inverse[...], prod[...], preferred_element_type=f32) * (1.0 / block)).astype(bf16)
    rows = outs[0].shape[0]
    mine = lax.rem(lax.axis_index("ctx"), GROUP)
    for d in range(GROUP):
        outs[d][...] = result[pl.ds(pl.multiple_of((mine ^ d) * rows, rows), rows), :]


def lag_half_kernel(by, a, b, mine, theirs):
    rows = mine.shape[0]
    side = lax.rem(lax.axis_index("ctx") // (GROUP * by), 2)
    for out, at in ((mine, side), (theirs, 1 - side)):
        at = pl.ds(pl.multiple_of(at * rows, rows), rows)
        out[...] = (a[at, :] + b[at, :].astype(f32)).astype(out.dtype)


def lag_sum_kernel(a, b, *outs):
    rows = outs[0].shape[0]
    low = lax.rem(lax.axis_index("ctx"), 2)
    for p in range(2):
        at = pl.ds(pl.multiple_of((low ^ p) * rows, rows), rows)
        outs[p][...] = a[at, :] + b[at, :].astype(f32)


def lag_place_kernel(a, b, out):
    part = a.shape[1]
    low = lax.rem(lax.axis_index("ctx"), 2)
    for p, ref in enumerate((a, b)):
        out[:, pl.ds(pl.multiple_of((low ^ p) * part, part), part)] = ref[...]


def finish_kernel(groups, chunks, which, *refs):
    pieces, (grad_out, values, x_one), refs = refs[:GROUP], refs[GROUP : GROUP + 3], refs[-8:]
    hbm, token, bufs, sems = refs[:3], refs[3], refs[4:7], refs[7]
    tok, chans = values.shape
    part = groups // GROUP
    mine = lax.rem(lax.axis_index("ctx"), GROUP)
    step = tok // chunks
    token[...] = jnp.zeros_like(token)

    def write(outs):
        copies = []
        for i in range(chunks):
            rows = slice(i * step, (i + 1) * step)
            for d in range(GROUP):
                for r in range(chans // groups):
                    cols = pl.ds(pl.multiple_of(r * groups + (mine ^ d) * part, part), part)
                    piece = pieces[d][rows, r * part : (r + 1) * part].astype(f32)
                    for a, gate in outs:
                        bufs[a][rows, cols] = (piece * gate[rows, cols].astype(f32)).astype(bf16)
            at = pl.ds(i * step, step)
            for a, _ in outs:
                copies.append(pltpu.make_async_copy(bufs[a].at[at], hbm[a].at[at], sems.at[a, i]))
                copies[-1].start()
        for copy in copies:
            copy.wait()

    is_grad = jnp.where(even_super(), 0, 1) == which
    pl.when(is_grad)(lambda: write([(0, values), (2, x_one)]))
    pl.when(jnp.logical_not(is_grad))(lambda: write([(1, grad_out)]))


def local(x_one, x_two, values, grad_out, filter_raw):
    tok, chans = x_one.shape
    tap_rows, own_filters = filter_raw.shape
    n, n_ch = lax.axis_size("ctx"), lax.axis_size("ch")
    taps, groups = tap_rows * n, own_filters * n_ch
    part = groups // GROUP
    repeat = chans // groups
    wide = repeat * part
    block = GROUP * tok
    span = taps // block
    assert span == 2 and taps % block == 0
    supers = n // GROUP
    scale = 1.0 / math.sqrt(taps)
    table, rest, inverse, inverse_rest = (jnp.asarray(t) for t in dft_tables(block))
    fast = n_ch == 2 and supers == 4 and taps // supers <= block

    def inside(value, d):
        return lax.ppermute(value, "ctx", [(i, i ^ d) for i in range(n)])

    def across(value, d):
        return lax.ppermute(value, "ctx", [(i, i ^ (d * GROUP)) for i in range(n)])

    def beside(value, odd):
        sides = [(i, ((i // GROUP - odd) ^ 1) + odd) for i in range(n) if i // GROUP >= odd]
        return lax.ppermute(value, "ctx", [(i, s * GROUP + i % GROUP) for i, s in sides if s < supers])

    def swap(value):
        return lax.ppermute(value, "ch", [(0, 1), (1, 0)])

    def trade(pieces):
        return [pieces[0]] + [inside(pieces[d], d) for d in range(1, GROUP)]

    chunks = 4
    in_hbm, in_vmem = pl.BlockSpec(memory_space=pltpu.HBM), pl.BlockSpec(memory_space=pltpu.VMEM)
    pieces_shape = [((tok, wide), bf16)] * GROUP
    block_shape = ((block, wide), bf16)

    gates = call(
        functools.partial(gate_kernel, groups, chunks),
        [((2 * tok, wide), bf16)] * GROUP,
        *(pltpu.with_memory_space_constraint(a, pltpu.HBM) for a in (x_one, values, grad_out, x_two)),
        scratch=[pltpu.VMEM((tok, chans), bf16)] * 4 + [pltpu.SemaphoreType.DMA((4, chunks))],
        specs=[in_hbm] * 4,
    )
    pieces = trade(gates)
    if fast:
        own_rows = call(pass_kernel, [(filter_raw.shape, bf16)], filter_raw, after=[pieces[1]])[0]
        raw = [own_rows] + [across(own_rows, d) for d in range(1, supers)]
        lower, upper, *cut = call(
            assemble_split_kernel,
            [block_shape, block_shape] + [((supers * tap_rows, part), bf16)] * 2,
            *pieces,
            *raw,
        )

        def to_users(value, p, q):
            pairs = []
            for i in range(n):
                j1, j0 = (i // 2) % 2, i % 2
                for x in range(2):
                    to = i // GROUP * GROUP + 2 * x + (p ^ j0)
                    pairs.append((i * 2 + x, to * 2 + (q ^ j1)))
            return lax.ppermute(value, ("ctx", "ch"), pairs)

        filt = [to_users(cut[p], p, q) for p in range(2) for q in range(2)]
    else:
        lower, upper = call(assemble_kernel, [block_shape, block_shape], *pieces)
        whole = lax.all_gather(filter_raw, "ctx", axis=0, tiled=True)
        whole = lax.all_gather(whole, "ch", axis=1, tiled=True)
        start = lax.rem(lax.axis_index("ctx"), GROUP) * part
        filt = [lax.dynamic_slice(whole, (0, start), (taps, part))]
    own, own_lag = call(
        own_kernel, [((2, 2 * block, wide), f32), ((2 * block, part), f32)], lower, upper, table
    )
    slab = taps // supers if fast else block
    weights = call(
        functools.partial(filter_spectra_kernel, scale, fast),
        [((3, 2 * block, part), f32)],
        *filt,
        table,
        rest,
        scratch=[pltpu.VMEM((taps // slab, slab, part), bf16)],
        after=[own_lag],
    )[0]
    one, two = beside(lower, 0), beside(upper, 1)
    passed = call(pass_kernel, [block_shape], two, after=[weights])[0]
    far_one, far_two = beside(passed, 0), beside(one, 1)
    near, *lags = call(
        functools.partial(lag_kernel, fast, scale),
        [((2, 2 * block, wide), f32)] + ([((taps // 2, part), t) for t in (f32, bf16)] if fast else [((taps, part), f32)]),
        one,
        two,
        own,
        own_lag,
        table,
        inverse,
        inverse_rest,
        scratch=[pltpu.VMEM((2 * block, 2 * part), bf16)] * 2 + [pltpu.VMEM((block, 2 * part), f32)],
        after=[weights],
    )

    def convolve(which, prior, far, *more):
        return call(
            functools.partial(conv_kernel, which),
            pieces_shape,
            far,
            near,
            own,
            weights,
            table,
            inverse,
            scratch=[
                pltpu.VMEM((2 * block, wide), f32),
                pltpu.VMEM((2 * block, wide), bf16),
                pltpu.VMEM((block, wide), bf16),
            ],
            after=[prior, *more],
        )

    def finish(pieces, prior, which, *others):
        return call(
            functools.partial(finish_kernel, groups, chunks, which),
            [((tok, chans), bf16)] * 3 + [((8, 128), f32)],
            *pieces,
            grad_out,
            values,
            x_one,
            *others,
            scratch=[pltpu.VMEM((tok, chans), bf16)] * 3 + [pltpu.SemaphoreType.DMA((3, chunks))],
            specs=[in_vmem] * (GROUP + 3) + [in_hbm] * len(others),
            out_specs=[in_hbm] * 3 + [in_vmem],
            aliases={GROUP + 3 + i: i for i in range(len(others))},
            after=[prior],
        )

    conv = convolve(0, lags[0], far_one)
    prior = conv[0]
    if fast:
        mine, theirs = lags
        mine, theirs = call(
            functools.partial(lag_half_kernel, 2),
            [((taps // 4, part), t) for t in (f32, bf16)],
            mine,
            swap(theirs),
            after=[prior],
        )
        prior = mine
    conv = trade(conv)
    back = convolve(1, prior, far_two, conv[1])
    prior = back[0]
    if fast:
        mine, theirs = call(
            functools.partial(lag_half_kernel, 1),
            [((taps // 8, part), t) for t in (f32, bf16)],
            mine,
            across(theirs, 2),
            after=[prior],
        )
        prior = mine
    *grads, prior = finish(conv, prior, 0)
    if fast:
        sums = call(
            lag_sum_kernel, [((tap_rows, part), f32)] * 2, mine, across(theirs, 1), after=[prior]
        )
        prior = sums[0]
    *grads, prior = finish(trade(back), prior, 1, *grads)
    if fast:

        def owner(value, p):
            pairs = []
            for i in range(n):
                j1, j0 = (i // 2) % 2, i % 2
                for x in range(2):
                    to = i // GROUP * GROUP + 2 * x + (p ^ j0)
                    pairs.append((i * 2 + x, to * 2 + j1))
            return lax.ppermute(value, ("ctx", "ch"), pairs)

        landed = [owner(s, p) for p, s in enumerate(sums)]
        grad_filter = call(lag_place_kernel, [((tap_rows, own_filters), f32)], *landed, after=[prior])[0]
    else:
        start = lax.rem(lax.axis_index("ctx"), GROUP) * part
        terms = lax.dynamic_update_slice(jnp.zeros((taps, groups), f32), lags[0], (0, start))
        by_taps = lax.psum_scatter(terms, "ctx", scatter_dimension=0, tiled=True)
        grad_filter = lax.psum_scatter(by_taps, "ch", scatter_dimension=1, tiled=True)
    return (*grads, grad_filter)


def solution(mesh):
    placed = P("ctx", "ch")
    return jax.shard_map(
        local,
        mesh=mesh,
        in_specs=(placed,) * 5,
        out_specs=(placed,) * 4,
        check_vma=False,
    )
```

```python
import functools
import math

import jax
import jax.numpy as jnp
import ml_dtypes
import numpy as np
from jax import lax
from jax.experimental import pallas as pl
from jax.experimental.pallas import tpu as pltpu
from jax.sharding import PartitionSpec as P

GROUP = 4
f32 = jnp.float32
bf16 = jnp.bfloat16
VMEM_LIMIT = 24 * 1024 * 1024
BINS = 64


def dft_tables(block):
    size = 2 * block
    place = np.arange(block)
    rows = []
    for parity in (0, 1):
        freq = np.arange(parity, block, 2)
        angle = 2.0 * math.pi / (2 * size) * ((2 * freq[:, None] + 1) * place[None, :] % (2 * size))
        rows += [np.cos(angle), -np.sin(angle)]
    table = np.concatenate(rows, axis=0)
    high = table.astype(ml_dtypes.bfloat16)
    rest = (table - high.astype(np.float64)).astype(ml_dtypes.bfloat16)
    return high, rest, np.ascontiguousarray(high.T)


def call(kernel, outs, *args, scratch=(), flops=0, specs=None, out_specs=None, after=(), aliases=None):
    bytes_accessed = sum(a.size * a.dtype.itemsize for a in args)
    bytes_accessed += sum(math.prod(s) * jnp.dtype(t).itemsize for s, t in outs)
    whole = pl.BlockSpec(memory_space=pltpu.VMEM)
    n_args, n_after = len(args), len(after)

    def run(*refs):
        kernel(*refs[:n_args], *refs[n_args + n_after :])

    return pl.pallas_call(
        run,
        out_shape=[jax.ShapeDtypeStruct(s, t) for s, t in outs],
        in_specs=(specs or [whole] * n_args) + [pl.BlockSpec(memory_space=pl.ANY)] * n_after,
        out_specs=out_specs or [whole] * len(outs),
        scratch_shapes=list(scratch),
        input_output_aliases=aliases or {},
        compiler_params=pltpu.CompilerParams(vmem_limit_bytes=VMEM_LIMIT),
        cost_estimate=pl.CostEstimate(flops=0, bytes_accessed=0, transcendentals=0),
    )(*args, *after)


def gate_kernel(groups, chunks, *refs):
    hbm, outs, bufs, sems = refs[:4], refs[4 : 4 + GROUP], refs[4 + GROUP : 8 + GROUP], refs[8 + GROUP]
    tok, chans = bufs[0].shape
    part = groups // GROUP
    mine = lax.rem(lax.axis_index("ctx"), GROUP)
    step = tok // chunks
    copies = []
    for s in (0, 2):
        for i in range(chunks):
            rows = pl.ds(i * step, step)
            copies.append(
                [pltpu.make_async_copy(hbm[a].at[rows], bufs[a].at[rows], sems.at[a, i]) for a in (s, s + 1)]
            )
            for copy in copies[-1]:
                copy.start()
    for s in range(2):
        for i in range(chunks):
            for copy in copies[s * chunks + i]:
                copy.wait()
            rows, to = slice(i * step, (i + 1) * step), slice(s * tok + i * step, s * tok + (i + 1) * step)
            for d in range(GROUP):
                for r in range(chans // groups):
                    at = pl.ds(pl.multiple_of(r * groups + (mine ^ d) * part, part), part)
                    prod = bufs[2 * s][rows, at].astype(f32) * bufs[2 * s + 1][rows, at].astype(f32)
                    outs[d][to, r * part : (r + 1) * part] = prod.astype(bf16)


def even_super():
    return lax.rem(lax.axis_index("ctx") // GROUP, 2) == 0


def assemble(pieces, lower, upper):
    rows = lower.shape[0] // GROUP
    mine = lax.rem(lax.axis_index("ctx"), GROUP)

    def place(p_out, g_out):
        for d in range(GROUP):
            at = pl.ds(pl.multiple_of((mine ^ d) * rows, rows), rows)
            p_out[at, :] = pieces[d][:rows, :]
            g_out[at, :] = pieces[d][rows:, :]

    even = even_super()
    pl.when(even)(lambda: place(lower, upper))
    pl.when(jnp.logical_not(even))(lambda: place(upper, lower))


def assemble_kernel(*refs):
    assemble(refs[:GROUP], *refs[GROUP:])


def assemble_split_kernel(*refs):
    pieces, raw, (lower, upper, *outs) = refs[:GROUP], refs[GROUP:-4], refs[-4:]
    assemble(pieces, lower, upper)
    sup, low = lax.axis_index("ctx") // GROUP, lax.rem(lax.axis_index("ctx"), 2)
    rows, part = raw[0].shape[0], outs[0].shape[1]
    for d, ref in enumerate(raw):
        at = pl.ds(pl.multiple_of((sup ^ d) * rows, rows), rows)
        for p in range(2):
            outs[p][at, :] = ref[:, pl.ds(pl.multiple_of((low ^ p) * part, part), part)]


def pass_kernel(*refs):
    n = len(refs) // 2
    for value, out in zip(refs[:n], refs[n:]):
        out[...] = value[...]


def filter_spectra_kernel(scale, fast, *refs):
    table_ref, rest_ref, out, taps_ref = refs[-4:]
    pieces = refs[:-4]
    n_slabs, slab, part = taps_ref.shape
    block = table_ref.shape[1]
    mine = lax.rem(lax.axis_index("ctx"), GROUP)
    for s in range(n_slabs):
        if fast:
            rows = slab // GROUP
            for d in range(GROUP):
                p, q = divmod(d, 2)
                member = (q ^ lax.axis_index("ch")) * 2 + (p ^ lax.rem(mine, 2))
                at = pl.ds(pl.multiple_of(member * rows, rows), rows)
                taps_ref[s, at, :] = pieces[d][s * rows : (s + 1) * rows, :]
        else:
            taps_ref[s] = pieces[0][s * slab : (s + 1) * slab, :]
    quarter = block // 2
    each = block // slab
    for k in range(n_slabs // each):
        spec = None
        for i in range(each):
            cols = slice(i * slab, (i + 1) * slab)
            for t in (table_ref, rest_ref):
                term = jnp.dot(t[:, cols], taps_ref[k * each + i], preferred_element_type=f32)
                spec = term if spec is None else spec + term
        spec = spec * scale
        for parity, sign in ((0, 1.0), (1, -1.0)):
            re = slice(parity * block, parity * block + quarter)
            im = slice(parity * block + quarter, (parity + 1) * block)
            if k == 0:
                out[0, re, :] = spec[re]
                out[0, im, :] = spec[im]
            else:
                out[k, re, :] += spec[re]
                out[k, im, :] += spec[im]
            out[k + 1, re, :] = -sign * spec[im]
            out[k + 1, im, :] = sign * spec[re]


def times(e_re, e_im, a_re, a_im):
    return e_re * a_re - e_im * a_im, e_re * a_im + e_im * a_re


def conj_times(e_re, e_im, a_re, a_im):
    return e_re * a_re + e_im * a_im, e_re * a_im - e_im * a_re


def bin_rows(block, visit):
    @pl.loop(0, 2)
    def _(parity):
        sign = 1.0 - 2.0 * parity.astype(f32)

        @pl.loop(0, block // 2 // BINS)
        def _(step):
            re = pl.multiple_of(parity * block + step * BINS, BINS)
            im = pl.multiple_of(parity * block + block // 2 + step * BINS, BINS)
            visit(sign, pl.ds(re, BINS), pl.ds(im, BINS))


def own_kernel(lower, upper, table, spec, lag):
    block, wide = lower.shape
    part = lag.shape[1]
    spec[0] = jnp.dot(table[...], lower[...], preferred_element_type=f32)
    spec[1] = jnp.dot(table[...], upper[...], preferred_element_type=f32)
    sign = jnp.where(even_super(), 1.0, -1.0).astype(f32)

    def visit(_, re, im):
        total = None
        for r in range(wide // part):
            cols = slice(r * part, (r + 1) * part)
            t = conj_times(spec[0, re, cols], spec[0, im, cols], spec[1, re, cols], spec[1, im, cols])
            total = t if total is None else (total[0] + t[0], total[1] + t[1])
        lag[re, :], lag[im, :] = total[0], total[1] * sign

    bin_rows(block, visit)


def lag_kernel(fast, scale, one, two, own, own_lag, table, inverse, spec, *refs):
    n_out = 2 if fast else 1
    lag_outs, (lag_prod, lag_result) = refs[:n_out], refs[n_out:]
    block, wide = one.shape
    part = own_lag.shape[1]
    spec[0] = jnp.dot(table[...], one[...], preferred_element_type=f32)
    spec[1] = jnp.dot(table[...], two[...], preferred_element_type=f32)
    at = jnp.where(even_super(), 1, 0)

    def visit(sign, re, im):
        lags = [(own_lag[re, :], own_lag[im, :]), None, None]
        for r in range(wide // part):
            cols = slice(r * part, (r + 1) * part)
            p1 = spec[at, re, cols], spec[at, im, cols]
            g1 = spec[1 - at, re, cols], spec[1 - at, im, cols]
            g0 = own[at, re, cols], own[at, im, cols]
            for k, (p, g) in ((1, (p1, g0)), (2, (p1, g1))):
                t = conj_times(*p, *g)
                lags[k] = t if lags[k] is None else (lags[k][0] + t[0], lags[k][1] + t[1])
        for k in range(2):
            cols = slice(k * part, (k + 1) * part)
            w_re = lags[k][0] + sign * lags[k + 1][1]
            w_im = lags[k][1] - sign * lags[k + 1][0]
            lag_prod[re, cols] = w_re.astype(bf16)
            lag_prod[im, cols] = w_im.astype(bf16)

    bin_rows(block, visit)
    lag_result[...] = jnp.dot(inverse[...], lag_prod[...], preferred_element_type=f32) * (scale / block)
    if fast:
        x = lax.axis_index("ch")
        keep, send = lag_outs
        piece = keep.shape[0] // (lax.axis_size("ctx") // GROUP)
        for s in range(keep.shape[0] // piece):
            i, low = divmod(2 * piece * s, block)
            cols = slice(i * part, (i + 1) * part)
            order = s // 2 + s % 2 * 2
            to = slice(order * piece, (order + 1) * piece)
            here = pl.ds(pl.multiple_of(low + x * piece, piece), piece)
            keep[to, :] = lag_result[here, cols]
            there = pl.ds(pl.multiple_of(low + (1 - x) * piece, piece), piece)
            send[to, :] = lag_result[there, cols].astype(bf16)
    else:
        for i in range(2):
            lag_outs[0][i * block : (i + 1) * block, :] = lag_result[:, i * part : (i + 1) * part]


def conv_kernel(which, far, near, own, weights, table, inverse, *refs):
    outs, (spec, prod, result) = refs[:GROUP], refs[GROUP:]
    block, wide = far.shape
    part = weights.shape[2]
    conj = jnp.where(even_super(), 1 - which, which)
    side = (1 - 2 * conj).astype(f32)
    spec[...] = jnp.dot(table[...], far[...], preferred_element_type=f32)

    def visit(_, re, im):
        e = [(weights[k, re, :], weights[k, im, :] * side) for k in range(3)]
        for r in range(wide // part):
            cols = slice(r * part, (r + 1) * part)
            total = times(*e[2], spec[re, cols], spec[im, cols])
            for k, ref, i in ((0, own, 1 - which), (1, near, which)):
                t = times(*e[k], ref[i, re, cols], ref[i, im, cols])
                total = total[0] + t[0], total[1] + t[1]
            prod[re, cols] = total[0].astype(bf16)
            prod[im, cols] = total[1].astype(bf16)

    bin_rows(block, visit)
    result[...] = (jnp.dot(inverse[...], prod[...], preferred_element_type=f32) * (1.0 / block)).astype(bf16)
    rows = outs[0].shape[0]
    mine = lax.rem(lax.axis_index("ctx"), GROUP)
    for d in range(GROUP):
        outs[d][...] = result[pl.ds(pl.multiple_of((mine ^ d) * rows, rows), rows), :]


def lag_add_kernel(a, b, out):
    out[...] = (a[...] + b[...].astype(f32)).astype(out.dtype)


def lag_half_kernel(by, *refs):
    terms, (mine, theirs) = refs[:-2], refs[-2:]
    rows = mine.shape[0]
    side = lax.rem(lax.axis_index("ctx") // (GROUP * by), 2)
    for out, at in ((mine, side), (theirs, 1 - side)):
        at = pl.ds(pl.multiple_of(at * rows, rows), rows)
        total = terms[0][at, :].astype(f32)
        for term in terms[1:]:
            total = total + term[at, :].astype(f32)
        out[...] = total.astype(out.dtype)


def lag_sum_kernel(a, b, *outs):
    rows = outs[0].shape[0]
    low = lax.rem(lax.axis_index("ctx"), 2)
    for p in range(2):
        at = pl.ds(pl.multiple_of((low ^ p) * rows, rows), rows)
        outs[p][...] = a[at, :] + b[at, :].astype(f32)


def lag_place_kernel(a, b, out):
    part = a.shape[1]
    low = lax.rem(lax.axis_index("ctx"), 2)
    for p, ref in enumerate((a, b)):
        out[:, pl.ds(pl.multiple_of((low ^ p) * part, part), part)] = ref[...]


def finish_kernel(groups, chunks, which, *refs):
    pieces, (grad_out, values, x_one), refs = refs[:GROUP], refs[GROUP : GROUP + 3], refs[-8:]
    hbm, token, bufs, sems = refs[:3], refs[3], refs[4:7], refs[7]
    tok, chans = values.shape
    part = groups // GROUP
    mine = lax.rem(lax.axis_index("ctx"), GROUP)
    step = tok // chunks
    token[...] = jnp.zeros_like(token)

    def write(outs):
        copies = []
        for i in range(chunks):
            rows = slice(i * step, (i + 1) * step)
            for d in range(GROUP):
                for r in range(chans // groups):
                    cols = pl.ds(pl.multiple_of(r * groups + (mine ^ d) * part, part), part)
                    piece = pieces[d][rows, r * part : (r + 1) * part].astype(f32)
                    for a, gate in outs:
                        bufs[a][rows, cols] = (piece * gate[rows, cols].astype(f32)).astype(bf16)
            at = pl.ds(i * step, step)
            for a, _ in outs:
                copies.append(pltpu.make_async_copy(bufs[a].at[at], hbm[a].at[at], sems.at[a, i]))
                copies[-1].start()
        for copy in copies:
            copy.wait()

    is_grad = jnp.where(even_super(), 0, 1) == which
    pl.when(is_grad)(lambda: write([(0, values), (2, x_one)]))
    pl.when(jnp.logical_not(is_grad))(lambda: write([(1, grad_out)]))


def local(x_one, x_two, values, grad_out, filter_raw):
    tok, chans = x_one.shape
    tap_rows, own_filters = filter_raw.shape
    n, n_ch = lax.axis_size("ctx"), lax.axis_size("ch")
    taps, groups = tap_rows * n, own_filters * n_ch
    part = groups // GROUP
    repeat = chans // groups
    wide = repeat * part
    block = GROUP * tok
    span = taps // block
    assert span == 2 and taps % block == 0
    supers = n // GROUP
    scale = 1.0 / math.sqrt(taps)
    table, rest, inverse = (jnp.asarray(t) for t in dft_tables(block))
    fast = n_ch == 2 and supers == 4 and taps // supers <= block

    def inside(value, d):
        return lax.ppermute(value, "ctx", [(i, i ^ d) for i in range(n)])

    def across(value, d):
        return lax.ppermute(value, "ctx", [(i, i ^ (d * GROUP)) for i in range(n)])

    def beside(value, odd):
        sides = [(i, ((i // GROUP - odd) ^ 1) + odd) for i in range(n) if i // GROUP >= odd]
        return lax.ppermute(value, "ctx", [(i, s * GROUP + i % GROUP) for i, s in sides if s < supers])

    def swap(value):
        return lax.ppermute(value, "ch", [(0, 1), (1, 0)])

    def trade(pieces):
        return [pieces[0]] + [inside(pieces[d], d) for d in range(1, GROUP)]

    chunks = 4
    in_hbm, in_vmem = pl.BlockSpec(memory_space=pltpu.HBM), pl.BlockSpec(memory_space=pltpu.VMEM)
    pieces_shape = [((tok, wide), bf16)] * GROUP
    block_shape = ((block, wide), bf16)

    gates = call(
        functools.partial(gate_kernel, groups, chunks),
        [((2 * tok, wide), bf16)] * GROUP,
        *(pltpu.with_memory_space_constraint(a, pltpu.HBM) for a in (x_one, values, grad_out, x_two)),
        scratch=[pltpu.VMEM((tok, chans), bf16)] * 4 + [pltpu.SemaphoreType.DMA((4, chunks))],
        specs=[in_hbm] * 4,
    )
    pieces = trade(gates)
    if fast:
        own_rows = call(pass_kernel, [(filter_raw.shape, bf16)], filter_raw, after=[pieces[1]])[0]
        raw = [own_rows] + [across(own_rows, d) for d in range(1, supers)]
        lower, upper, *cut = call(
            assemble_split_kernel,
            [block_shape, block_shape] + [((supers * tap_rows, part), bf16)] * 2,
            *pieces,
            *raw,
        )

        def to_users(value, p, q):
            pairs = []
            for i in range(n):
                j1, j0 = (i // 2) % 2, i % 2
                for x in range(2):
                    to = i // GROUP * GROUP + 2 * x + (p ^ j0)
                    pairs.append((i * 2 + x, to * 2 + (q ^ j1)))
            return lax.ppermute(value, ("ctx", "ch"), pairs)

        filt = [to_users(cut[p], p, q) for p in range(2) for q in range(2)]
    else:
        lower, upper = call(assemble_kernel, [block_shape, block_shape], *pieces)
        whole = lax.all_gather(filter_raw, "ctx", axis=0, tiled=True)
        whole = lax.all_gather(whole, "ch", axis=1, tiled=True)
        start = lax.rem(lax.axis_index("ctx"), GROUP) * part
        filt = [lax.dynamic_slice(whole, (0, start), (taps, part))]
    own, own_lag = call(
        own_kernel, [((2, 2 * block, wide), f32), ((2 * block, part), f32)], lower, upper, table
    )
    slab = taps // supers if fast else block
    weights = call(
        functools.partial(filter_spectra_kernel, scale, fast),
        [((3, 2 * block, part), f32)],
        *filt,
        table,
        rest,
        scratch=[pltpu.VMEM((taps // slab, slab, part), bf16)],
        after=[own_lag],
    )[0]
    one, two = beside(lower, 0), beside(upper, 1)
    pass_two, pass_one = call(pass_kernel, [block_shape] * 2, two, one, after=[weights])
    far_one, far_two = beside(pass_two, 0), beside(pass_one, 1)
    near, *lags = call(
        functools.partial(lag_kernel, fast, scale),
        [((2, 2 * block, wide), f32)] + ([((taps // 2, part), t) for t in (f32, bf16)] if fast else [((taps, part), f32)]),
        one,
        two,
        own,
        own_lag,
        table,
        inverse,
        scratch=[pltpu.VMEM((2 * block, 2 * part), bf16), pltpu.VMEM((block, 2 * part), f32)],
        after=[weights],
    )

    def convolve(which, prior, far, *more):
        return call(
            functools.partial(conv_kernel, which),
            pieces_shape,
            far,
            near,
            own,
            weights,
            table,
            inverse,
            scratch=[
                pltpu.VMEM((2 * block, wide), f32),
                pltpu.VMEM((2 * block, wide), bf16),
                pltpu.VMEM((block, wide), bf16),
            ],
            after=[prior, *more],
        )

    def finish(pieces, prior, which, *others):
        return call(
            functools.partial(finish_kernel, groups, chunks, which),
            [((tok, chans), bf16)] * 3 + [((8, 128), f32)],
            *pieces,
            grad_out,
            values,
            x_one,
            *others,
            scratch=[pltpu.VMEM((tok, chans), bf16)] * 3 + [pltpu.SemaphoreType.DMA((3, chunks))],
            specs=[in_vmem] * (GROUP + 3) + [in_hbm] * len(others),
            out_specs=[in_hbm] * 3 + [in_vmem],
            aliases={GROUP + 3 + i: i for i in range(len(others))},
            after=[prior],
        )

    prior = lags[0]
    if fast:
        total = call(lag_add_kernel, [((taps // 2, part), bf16)], lags[0], swap(lags[1]))[0]
        prior = total
        turned = []
        for i in range(n):
            for x in range(2):
                to = i // GROUP * GROUP + 2 * x + i % 2
                turned.append((i * 2 + x, to * 2 + (i // 2) % 2))
        total = lax.ppermute(total, ("ctx", "ch"), turned)
    conv = convolve(0, prior, far_one)
    prior = conv[0]
    conv = trade(conv)
    back = convolve(1, prior, far_two)
    prior = back[0]
    back = trade(back)
    if fast:
        mine, theirs = call(
            functools.partial(lag_half_kernel, 1),
            [((taps // 4, part), t) for t in (f32, bf16)],
            total,
            after=[prior],
        )
        prior = mine
    *grads, prior = finish(conv, prior, 0)
    if fast:
        mine, theirs = call(
            functools.partial(lag_half_kernel, 2),
            [((taps // 8, part), t) for t in (f32, bf16)],
            mine,
            across(theirs, 1),
            after=[prior],
        )
        prior = mine
    if fast:
        sums = call(
            lag_sum_kernel, [((tap_rows, part), f32)] * 2, mine, across(theirs, 2), after=[prior]
        )
        prior = sums[0]
    *grads, prior = finish(back, prior, 1, *grads)
    if fast:

        landed = [sums[0], inside(sums[1], 1)]
        grad_filter = call(lag_place_kernel, [((tap_rows, own_filters), f32)], *landed, after=[prior])[0]
    else:
        start = lax.rem(lax.axis_index("ctx"), GROUP) * part
        terms = lax.dynamic_update_slice(jnp.zeros((taps, groups), f32), lags[0], (0, start))
        by_taps = lax.psum_scatter(terms, "ctx", scatter_dimension=0, tiled=True)
        grad_filter = lax.psum_scatter(by_taps, "ch", scatter_dimension=1, tiled=True)
    return (*grads, grad_filter)


def solution(mesh):
    placed = P("ctx", "ch")
    return jax.shard_map(
        local,
        mesh=mesh,
        in_specs=(placed,) * 5,
        out_specs=(placed,) * 4,
        check_vma=False,
    )
```

```python
import functools
import math

import jax
import jax.numpy as jnp
import ml_dtypes
import numpy as np
from jax import lax
from jax.experimental import pallas as pl
from jax.experimental.pallas import tpu as pltpu
from jax.sharding import PartitionSpec as P

GROUP = 4
f32 = jnp.float32
bf16 = jnp.bfloat16
VMEM_LIMIT = 24 * 1024 * 1024
BINS = 128


def dft_tables(block):
    size = 2 * block
    place = np.arange(block)
    rows = []
    for parity in (0, 1):
        freq = np.arange(parity, block, 2)
        angle = 2.0 * math.pi / (2 * size) * ((2 * freq[:, None] + 1) * place[None, :] % (2 * size))
        rows += [np.cos(angle), -np.sin(angle)]
    table = np.concatenate(rows, axis=0)
    high = table.astype(ml_dtypes.bfloat16)
    rest = (table - high.astype(np.float64)).astype(ml_dtypes.bfloat16)
    return high, rest, np.ascontiguousarray(high.T)


def call(kernel, outs, *args, scratch=(), flops=0, specs=None, out_specs=None, after=(), aliases=None):
    bytes_accessed = sum(a.size * a.dtype.itemsize for a in args)
    bytes_accessed += sum(math.prod(s) * jnp.dtype(t).itemsize for s, t in outs)
    whole = pl.BlockSpec(memory_space=pltpu.VMEM)
    n_args, n_after = len(args), len(after)

    def run(*refs):
        kernel(*refs[:n_args], *refs[n_args + n_after :])

    return pl.pallas_call(
        run,
        out_shape=[jax.ShapeDtypeStruct(s, t) for s, t in outs],
        in_specs=(specs or [whole] * n_args) + [pl.BlockSpec(memory_space=pl.ANY)] * n_after,
        out_specs=out_specs or [whole] * len(outs),
        scratch_shapes=list(scratch),
        input_output_aliases=aliases or {},
        compiler_params=pltpu.CompilerParams(vmem_limit_bytes=VMEM_LIMIT),
        cost_estimate=pl.CostEstimate(flops=0, bytes_accessed=0, transcendentals=0),
    )(*args, *after)


def gate_kernel(groups, chunks, *refs):
    hbm, outs, bufs, sems = refs[:4], refs[4 : 4 + GROUP], refs[4 + GROUP : 8 + GROUP], refs[8 + GROUP]
    tok, chans = bufs[0].shape
    part = groups // GROUP
    mine = lax.rem(lax.axis_index("ctx"), GROUP)
    step = tok // chunks
    copies = []
    for s in (0, 2):
        for i in range(chunks):
            rows = pl.ds(i * step, step)
            copies.append(
                [pltpu.make_async_copy(hbm[a].at[rows], bufs[a].at[rows], sems.at[a, i]) for a in (s, s + 1)]
            )
            for copy in copies[-1]:
                copy.start()
    for s in range(2):
        for i in range(chunks):
            for copy in copies[s * chunks + i]:
                copy.wait()
            rows, to = slice(i * step, (i + 1) * step), slice(s * tok + i * step, s * tok + (i + 1) * step)
            for d in range(GROUP):
                for r in range(chans // groups):
                    at = pl.ds(pl.multiple_of(r * groups + (mine ^ d) * part, part), part)
                    prod = bufs[2 * s][rows, at].astype(f32) * bufs[2 * s + 1][rows, at].astype(f32)
                    outs[d][to, r * part : (r + 1) * part] = prod.astype(bf16)


def even_super():
    return lax.rem(lax.axis_index("ctx") // GROUP, 2) == 0


def assemble(pieces, lower, upper):
    rows = lower.shape[0] // GROUP
    mine = lax.rem(lax.axis_index("ctx"), GROUP)

    def place(p_out, g_out):
        for d in range(GROUP):
            at = pl.ds(pl.multiple_of((mine ^ d) * rows, rows), rows)
            p_out[at, :] = pieces[d][:rows, :]
            g_out[at, :] = pieces[d][rows:, :]

    even = even_super()
    pl.when(even)(lambda: place(lower, upper))
    pl.when(jnp.logical_not(even))(lambda: place(upper, lower))


def assemble_kernel(*refs):
    assemble(refs[:GROUP], *refs[GROUP:])


def assemble_split_kernel(*refs):
    pieces, raw, (lower, upper, *outs) = refs[:GROUP], refs[GROUP:-4], refs[-4:]
    assemble(pieces, lower, upper)
    sup, low = lax.axis_index("ctx") // GROUP, lax.rem(lax.axis_index("ctx"), 2)
    rows, part = raw[0].shape[0], outs[0].shape[1]
    for d, ref in enumerate(raw):
        at = pl.ds(pl.multiple_of((sup ^ d) * rows, rows), rows)
        for p in range(2):
            outs[p][at, :] = ref[:, pl.ds(pl.multiple_of((low ^ p) * part, part), part)]


def pass_kernel(*refs):
    n = len(refs) // 2
    for value, out in zip(refs[:n], refs[n:]):
        out[...] = value[...]


def filter_spectra_kernel(scale, fast, *refs):
    table_ref, rest_ref, out, taps_ref = refs[-4:]
    pieces = refs[:-4]
    n_slabs, slab, part = taps_ref.shape
    block = table_ref.shape[1]
    mine = lax.rem(lax.axis_index("ctx"), GROUP)
    for s in range(n_slabs):
        if fast:
            rows = slab // GROUP
            for d in range(GROUP):
                p, q = divmod(d, 2)
                member = (q ^ lax.axis_index("ch")) * 2 + (p ^ lax.rem(mine, 2))
                at = pl.ds(pl.multiple_of(member * rows, rows), rows)
                taps_ref[s, at, :] = pieces[d][s * rows : (s + 1) * rows, :]
        else:
            taps_ref[s] = pieces[0][s * slab : (s + 1) * slab, :]
    quarter = block // 2
    each = block // slab
    for k in range(n_slabs // each):
        spec = None
        for i in range(each):
            cols = slice(i * slab, (i + 1) * slab)
            for t in (table_ref, rest_ref):
                term = jnp.dot(t[:, cols], taps_ref[k * each + i], preferred_element_type=f32)
                spec = term if spec is None else spec + term
        spec = spec * scale
        for parity, sign in ((0, 1.0), (1, -1.0)):
            re = slice(parity * block, parity * block + quarter)
            im = slice(parity * block + quarter, (parity + 1) * block)
            if k == 0:
                out[0, re, :] = spec[re]
                out[0, im, :] = spec[im]
            else:
                out[k, re, :] += spec[re]
                out[k, im, :] += spec[im]
            out[k + 1, re, :] = -sign * spec[im]
            out[k + 1, im, :] = sign * spec[re]


def times(e_re, e_im, a_re, a_im):
    return e_re * a_re - e_im * a_im, e_re * a_im + e_im * a_re


def conj_times(e_re, e_im, a_re, a_im):
    return e_re * a_re + e_im * a_im, e_re * a_im - e_im * a_re


def bin_rows(block, visit):
    @pl.loop(0, 2)
    def _(parity):
        sign = 1.0 - 2.0 * parity.astype(f32)

        @pl.loop(0, block // 2 // BINS)
        def _(step):
            re = pl.multiple_of(parity * block + step * BINS, BINS)
            im = pl.multiple_of(parity * block + block // 2 + step * BINS, BINS)
            visit(sign, pl.ds(re, BINS), pl.ds(im, BINS))


def own_kernel(lower, upper, table, spec, lag):
    block, wide = lower.shape
    part = lag.shape[1]
    spec[0] = jnp.dot(table[...], lower[...], preferred_element_type=f32)
    spec[1] = jnp.dot(table[...], upper[...], preferred_element_type=f32)
    sign = jnp.where(even_super(), 1.0, -1.0).astype(f32)

    def visit(_, re, im):
        total = None
        for r in range(wide // part):
            cols = slice(r * part, (r + 1) * part)
            t = conj_times(spec[0, re, cols], spec[0, im, cols], spec[1, re, cols], spec[1, im, cols])
            total = t if total is None else (total[0] + t[0], total[1] + t[1])
        lag[re, :], lag[im, :] = total[0], total[1] * sign

    bin_rows(block, visit)


def lag_kernel(fast, scale, one, two, own, own_lag, table, inverse, spec, *refs):
    n_out = 2 if fast else 1
    lag_outs, (lag_prod, lag_result) = refs[:n_out], refs[n_out:]
    block, wide = one.shape
    part = own_lag.shape[1]
    spec[0] = jnp.dot(table[...], one[...], preferred_element_type=f32)
    spec[1] = jnp.dot(table[...], two[...], preferred_element_type=f32)
    at = jnp.where(even_super(), 1, 0)

    def visit(sign, re, im):
        lags = [(own_lag[re, :], own_lag[im, :]), None, None]
        for r in range(wide // part):
            cols = slice(r * part, (r + 1) * part)
            p1 = spec[at, re, cols], spec[at, im, cols]
            g1 = spec[1 - at, re, cols], spec[1 - at, im, cols]
            g0 = own[at, re, cols], own[at, im, cols]
            for k, (p, g) in ((1, (p1, g0)), (2, (p1, g1))):
                t = conj_times(*p, *g)
                lags[k] = t if lags[k] is None else (lags[k][0] + t[0], lags[k][1] + t[1])
        for k in range(2):
            cols = slice(k * part, (k + 1) * part)
            w_re = lags[k][0] + sign * lags[k + 1][1]
            w_im = lags[k][1] - sign * lags[k + 1][0]
            lag_prod[re, cols] = w_re.astype(bf16)
            lag_prod[im, cols] = w_im.astype(bf16)

    bin_rows(block, visit)
    lag_result[...] = jnp.dot(inverse[...], lag_prod[...], preferred_element_type=f32) * (scale / block)
    if fast:
        x = lax.axis_index("ch")
        keep, send = lag_outs
        piece = keep.shape[0] // (lax.axis_size("ctx") // GROUP)
        for s in range(keep.shape[0] // piece):
            i, low = divmod(2 * piece * s, block)
            cols = slice(i * part, (i + 1) * part)
            order = s // 2 + s % 2 * 2
            to = slice(order * piece, (order + 1) * piece)
            here = pl.ds(pl.multiple_of(low + x * piece, piece), piece)
            keep[to, :] = lag_result[here, cols]
            there = pl.ds(pl.multiple_of(low + (1 - x) * piece, piece), piece)
            send[to, :] = lag_result[there, cols].astype(bf16)
    else:
        for i in range(2):
            lag_outs[0][i * block : (i + 1) * block, :] = lag_result[:, i * part : (i + 1) * part]


def conv_kernel(which, far, near, own, weights, table, inverse, *refs):
    outs, (spec, prod, result) = refs[:GROUP], refs[GROUP:]
    block, wide = far.shape
    part = weights.shape[2]
    conj = jnp.where(even_super(), 1 - which, which)
    side = (1 - 2 * conj).astype(f32)
    spec[...] = jnp.dot(table[...], far[...], preferred_element_type=f32)

    def visit(_, re, im):
        e = [(weights[k, re, :], weights[k, im, :] * side) for k in range(3)]
        for r in range(wide // part):
            cols = slice(r * part, (r + 1) * part)
            total = times(*e[2], spec[re, cols], spec[im, cols])
            for k, ref, i in ((0, own, 1 - which), (1, near, which)):
                t = times(*e[k], ref[i, re, cols], ref[i, im, cols])
                total = total[0] + t[0], total[1] + t[1]
            prod[re, cols] = total[0].astype(bf16)
            prod[im, cols] = total[1].astype(bf16)

    bin_rows(block, visit)
    result[...] = (jnp.dot(inverse[...], prod[...], preferred_element_type=f32) * (1.0 / block)).astype(bf16)
    rows = outs[0].shape[0]
    mine = lax.rem(lax.axis_index("ctx"), GROUP)
    for d in range(GROUP):
        outs[d][...] = result[pl.ds(pl.multiple_of((mine ^ d) * rows, rows), rows), :]


def lag_add_kernel(a, b, out):
    out[...] = (a[...] + b[...].astype(f32)).astype(out.dtype)


def lag_half_kernel(by, *refs):
    terms, (mine, theirs) = refs[:-2], refs[-2:]
    rows = mine.shape[0]
    side = lax.rem(lax.axis_index("ctx") // (GROUP * by), 2)
    for out, at in ((mine, side), (theirs, 1 - side)):
        at = pl.ds(pl.multiple_of(at * rows, rows), rows)
        total = terms[0][at, :].astype(f32)
        for term in terms[1:]:
            total = total + term[at, :].astype(f32)
        out[...] = total.astype(out.dtype)


def lag_sum_kernel(a, b, *outs):
    rows = outs[0].shape[0]
    low = lax.rem(lax.axis_index("ctx"), 2)
    for p in range(2):
        at = pl.ds(pl.multiple_of((low ^ p) * rows, rows), rows)
        outs[p][...] = a[at, :] + b[at, :].astype(f32)


def lag_place_kernel(a, b, out):
    part = a.shape[1]
    low = lax.rem(lax.axis_index("ctx"), 2)
    for p, ref in enumerate((a, b)):
        out[:, pl.ds(pl.multiple_of((low ^ p) * part, part), part)] = ref[...]


def finish_kernel(groups, chunks, which, *refs):
    pieces, (grad_out, values, x_one), refs = refs[:GROUP], refs[GROUP : GROUP + 3], refs[-8:]
    hbm, token, bufs, sems = refs[:3], refs[3], refs[4:7], refs[7]
    tok, chans = values.shape
    part = groups // GROUP
    mine = lax.rem(lax.axis_index("ctx"), GROUP)
    step = tok // chunks
    token[...] = jnp.zeros_like(token)

    def write(outs):
        copies = []
        for i in range(chunks):
            rows = slice(i * step, (i + 1) * step)
            for d in range(GROUP):
                for r in range(chans // groups):
                    cols = pl.ds(pl.multiple_of(r * groups + (mine ^ d) * part, part), part)
                    piece = pieces[d][rows, r * part : (r + 1) * part].astype(f32)
                    for a, gate in outs:
                        bufs[a][rows, cols] = (piece * gate[rows, cols].astype(f32)).astype(bf16)
            at = pl.ds(i * step, step)
            for a, _ in outs:
                copies.append(pltpu.make_async_copy(bufs[a].at[at], hbm[a].at[at], sems.at[a, i]))
                copies[-1].start()
        for copy in copies:
            copy.wait()

    is_grad = jnp.where(even_super(), 0, 1) == which
    pl.when(is_grad)(lambda: write([(0, values), (2, x_one)]))
    pl.when(jnp.logical_not(is_grad))(lambda: write([(1, grad_out)]))


def local(x_one, x_two, values, grad_out, filter_raw):
    tok, chans = x_one.shape
    tap_rows, own_filters = filter_raw.shape
    n, n_ch = lax.axis_size("ctx"), lax.axis_size("ch")
    taps, groups = tap_rows * n, own_filters * n_ch
    part = groups // GROUP
    repeat = chans // groups
    wide = repeat * part
    block = GROUP * tok
    span = taps // block
    assert span == 2 and taps % block == 0
    supers = n // GROUP
    scale = 1.0 / math.sqrt(taps)
    table, rest, inverse = (jnp.asarray(t) for t in dft_tables(block))
    fast = n_ch == 2 and supers == 4 and taps // supers <= block

    def inside(value, d):
        return lax.ppermute(value, "ctx", [(i, i ^ d) for i in range(n)])

    def across(value, d):
        return lax.ppermute(value, "ctx", [(i, i ^ (d * GROUP)) for i in range(n)])

    def beside(value, odd):
        sides = [(i, ((i // GROUP - odd) ^ 1) + odd) for i in range(n) if i // GROUP >= odd]
        return lax.ppermute(value, "ctx", [(i, s * GROUP + i % GROUP) for i, s in sides if s < supers])

    def swap(value):
        return lax.ppermute(value, "ch", [(0, 1), (1, 0)])

    def trade(pieces):
        moved = {d: inside(pieces[d], d) for d in (2, 3, 1)}
        return [pieces[0]] + [moved[d] for d in range(1, GROUP)]

    chunks = 4
    in_hbm, in_vmem = pl.BlockSpec(memory_space=pltpu.HBM), pl.BlockSpec(memory_space=pltpu.VMEM)
    pieces_shape = [((tok, wide), bf16)] * GROUP
    block_shape = ((block, wide), bf16)

    gates = call(
        functools.partial(gate_kernel, groups, chunks),
        [((2 * tok, wide), bf16)] * GROUP,
        *(pltpu.with_memory_space_constraint(a, pltpu.HBM) for a in (x_one, values, grad_out, x_two)),
        scratch=[pltpu.VMEM((tok, chans), bf16)] * 4 + [pltpu.SemaphoreType.DMA((4, chunks))],
        specs=[in_hbm] * 4,
    )
    pieces = trade(gates)
    if fast:
        own_rows = call(pass_kernel, [(filter_raw.shape, bf16)], filter_raw, after=[pieces[1]])[0]
        raw = [own_rows] + [across(own_rows, d) for d in range(1, supers)]
        lower, upper, *cut = call(
            assemble_split_kernel,
            [block_shape, block_shape] + [((supers * tap_rows, part), bf16)] * 2,
            *pieces,
            *raw,
        )

        def to_users(value, p, q):
            pairs = []
            for i in range(n):
                j1, j0 = (i // 2) % 2, i % 2
                for x in range(2):
                    to = i // GROUP * GROUP + 2 * x + (p ^ j0)
                    pairs.append((i * 2 + x, to * 2 + (q ^ j1)))
            return lax.ppermute(value, ("ctx", "ch"), pairs)

        filt = [to_users(cut[p], p, q) for p in range(2) for q in range(2)]
    else:
        lower, upper = call(assemble_kernel, [block_shape, block_shape], *pieces)
        whole = lax.all_gather(filter_raw, "ctx", axis=0, tiled=True)
        whole = lax.all_gather(whole, "ch", axis=1, tiled=True)
        start = lax.rem(lax.axis_index("ctx"), GROUP) * part
        filt = [lax.dynamic_slice(whole, (0, start), (taps, part))]
    own, own_lag = call(
        own_kernel, [((2, 2 * block, wide), f32), ((2 * block, part), f32)], lower, upper, table
    )
    slab = taps // supers if fast else block
    weights = call(
        functools.partial(filter_spectra_kernel, scale, fast),
        [((3, 2 * block, part), f32)],
        *filt,
        table,
        rest,
        scratch=[pltpu.VMEM((taps // slab, slab, part), bf16)],
        after=[own_lag],
    )[0]
    one, two = beside(lower, 0), beside(upper, 1)
    pass_two, pass_one = call(pass_kernel, [block_shape] * 2, two, one, after=[weights])
    far_one, far_two = beside(pass_two, 0), beside(pass_one, 1)
    near, *lags = call(
        functools.partial(lag_kernel, fast, scale),
        [((2, 2 * block, wide), f32)] + ([((taps // 2, part), t) for t in (f32, bf16)] if fast else [((taps, part), f32)]),
        one,
        two,
        own,
        own_lag,
        table,
        inverse,
        scratch=[pltpu.VMEM((2 * block, 2 * part), bf16), pltpu.VMEM((block, 2 * part), f32)],
    )

    def convolve(which, prior, far, *more):
        return call(
            functools.partial(conv_kernel, which),
            pieces_shape,
            far,
            near,
            own,
            weights,
            table,
            inverse,
            scratch=[
                pltpu.VMEM((2 * block, wide), f32),
                pltpu.VMEM((2 * block, wide), bf16),
                pltpu.VMEM((block, wide), bf16),
            ],
            after=[prior, *more],
        )

    def finish(pieces, prior, which, *others):
        return call(
            functools.partial(finish_kernel, groups, chunks, which),
            [((tok, chans), bf16)] * 3 + [((8, 128), f32)],
            *pieces,
            grad_out,
            values,
            x_one,
            *others,
            scratch=[pltpu.VMEM((tok, chans), bf16)] * 3 + [pltpu.SemaphoreType.DMA((3, chunks))],
            specs=[in_vmem] * (GROUP + 3) + [in_hbm] * len(others),
            out_specs=[in_hbm] * 3 + [in_vmem],
            aliases={GROUP + 3 + i: i for i in range(len(others))},
            after=[prior],
        )

    prior = lags[0]
    if fast:
        total = call(lag_add_kernel, [((taps // 2, part), bf16)], lags[0], swap(lags[1]))[0]
        prior = total
        turned = []
        for i in range(n):
            for x in range(2):
                to = i // GROUP * GROUP + 2 * x + i % 2
                turned.append((i * 2 + x, to * 2 + (i // 2) % 2))
        total = lax.ppermute(total, ("ctx", "ch"), turned)
    conv = convolve(0, prior, far_one)
    prior = conv[0]
    conv = trade(conv)
    back = convolve(1, prior, far_two)
    prior = back[0]
    back = trade(back)
    if fast:
        mine, theirs = call(
            functools.partial(lag_half_kernel, 1),
            [((taps // 4, part), t) for t in (f32, bf16)],
            total,
            after=[prior],
        )
        prior = mine
    *grads, prior = finish(conv, prior, 0)
    if fast:
        mine, theirs = call(
            functools.partial(lag_half_kernel, 2),
            [((taps // 8, part), t) for t in (f32, bf16)],
            mine,
            across(theirs, 1),
            after=[prior],
        )
        prior = mine
    if fast:
        sums = call(
            lag_sum_kernel, [((tap_rows, part), f32)] * 2, mine, across(theirs, 2), after=[prior]
        )
        prior = sums[0]
    *grads, prior = finish(back, prior, 1, *grads)
    if fast:

        landed = [sums[0], inside(sums[1], 1)]
        grad_filter = call(lag_place_kernel, [((tap_rows, own_filters), f32)], *landed, after=[prior])[0]
    else:
        start = lax.rem(lax.axis_index("ctx"), GROUP) * part
        terms = lax.dynamic_update_slice(jnp.zeros((taps, groups), f32), lags[0], (0, start))
        by_taps = lax.psum_scatter(terms, "ctx", scatter_dimension=0, tiled=True)
        grad_filter = lax.psum_scatter(by_taps, "ch", scatter_dimension=1, tiled=True)
    return (*grads, grad_filter)


def solution(mesh):
    placed = P("ctx", "ch")
    return jax.shard_map(
        local,
        mesh=mesh,
        in_specs=(placed,) * 5,
        out_specs=(placed,) * 4,
        check_vma=False,
    )
```
